128 devices in a mesh: rep: 4 (over x_lo, core), fsdp: 32 (over z, y, x_hi).
Axes of the slice: x: 4 (x_hi: 2, x_lo: 2; x = x_hi * 2 + x_lo), y: 4, z: 4, core: 2. Of those that a mesh axis runs over, the one named last changes fastest.
Arguments:
- tokens: bfloat16 [4, 32768, 5120], P('rep', 'fsdp'), may hold values from -6 to 6
- targets: int32 [4, 32768], P('rep', 'fsdp'), may hold values from 0 to 1023
- norm_gain: float32 [5120], replicated, may hold values from 0.5 to 1.5
- weights: float32 [4, 5120, 1024], P('rep', 'fsdp'), may hold values from -6 to 6
- anchor: float32 [5120, 1024], P('fsdp', 'rep'), may hold values from -6 to 6
- momentum: float32 [5120, 1024], P('fsdp', 'rep'), may hold values from -2 to 2
- step_index: int32 [1], replicated, may hold values from 0 to 99999
- frag_table: int32 [8], replicated, may hold values from 0 to 7, each once
Outputs:
- token_loss: float32 [4, 32768], P('rep', 'fsdp')
- weights_out: float32 [4, 5120, 1024], P('rep', 'fsdp')
- momentum_out: float32 [5120, 1024], P('fsdp', 'rep')
The draws below stay inside these ranges and needn't reach their ends.
All inputs are finite; a program needn't handle non-finite values.
Results may differ from the reference program's by a relative error of at most 0.0025.
Values may be sent and summed in bfloat16 or wider, within the bound.
A program may use at most 128 MiB of HBM per device.

```python
import math
import jax
import jax.numpy as jnp
import numpy as np
from jax import lax

D = 5120
V = 1024
FRAGS = 8
TOK_DEV = 1024
REPS = 4
TOK_REP = 32768
FRAG_ROWS = 20


def with_ends(array, stream_key, low, high):
    longest = array.shape.index(max(array.shape))
    spots = []
    for shift in (0, 1):
        where = [jax.random.randint(jax.random.fold_in(stream_key, axis), (), 0, length) for axis, length in enumerate(array.shape)]
        where[longest] = (where[longest] + shift) % array.shape[longest]
        spots.append(tuple(where))
    return array.at[spots[0]].set(low).at[spots[1]].set(high)


def block_levels(stream_key, extent, split, smallest, top_value):
    def one(dim, blocks):
        heights = jax.random.uniform(jax.random.fold_in(jax.random.fold_in(stream_key, 6), dim), (blocks,), jnp.float32, smallest / len(split), top_value / len(split))
        return jnp.repeat(jnp.exp(heights), extent[dim] // blocks).reshape((-1,) + (1,) * (len(extent) - dim - 1))

    factor_of = one(*split[0])
    for cut in split[1:]:
        factor_of = factor_of * one(*cut)
    return factor_of


def rank_table(number_of, lean):
    portions = [(1 << 20) // math.isqrt(rank ** lean) + 1 for rank in range(1, number_of + 1)]
    deviation = 1 + sum(portions) // (1 << 30)
    return np.cumsum(np.array([max(1, weight // deviation) for weight in portions]))


def ranked(own_key, shape, amount, lean):
    table = rank_table(amount, lean)
    ticket = jax.random.randint(jax.random.fold_in(own_key, 1), shape, 0, int(table[amount - 1]))
    grade = jnp.searchsorted(jnp.asarray(table, jnp.int32), ticket, side="right")
    return jax.random.permutation(jax.random.fold_in(own_key, 2), amount)[grade].astype(jnp.int32)


def noise(stream_key, shape, deviation, most, pieces=(), kind=jnp.bfloat16):
    entries = deviation * jax.random.normal(stream_key, shape, jnp.float32)
    if pieces:
        entries = entries * block_levels(stream_key, shape, pieces, -0.22, 0.18)
    return jnp.clip(entries, -most, most).astype(kind)


def setup_inputs(seed: int = 0) -> dict:
    seeds = jax.random.split(jax.random.key(seed), 9)
    tokens = noise(seeds[0], (REPS, TOK_REP, D), 1.0, 6.0, ((0, 4), (1, 32)))
    targets = with_ends(ranked(seeds[1], (REPS, TOK_REP), V, 2), jax.random.fold_in(seeds[1], 3), 0, V - 1).astype(jnp.int32)
    norm_gain = jnp.clip(1.0 + 0.1 * jax.random.normal(seeds[2], (D,), jnp.float32), 0.5, 1.5)
    weights = noise(seeds[3], (REPS, D, V), 1.0, 6.0, ((0, 4), (1, 32)), jnp.float32)
    anchor = noise(seeds[4], (D, V), 1.0, 6.0, ((0, 32), (1, 4)), jnp.float32)
    momentum = noise(seeds[5], (D, V), 0.3, 2.0, ((0, 32), (1, 4)), jnp.float32)
    step_index = jax.random.randint(seeds[6], (1,), 0, 100000).astype(jnp.int32)
    frag_table = jax.random.permutation(seeds[7], FRAGS).astype(jnp.int32)
    return dict(tokens=tokens, targets=targets, norm_gain=norm_gain, weights=weights, anchor=anchor, momentum=momentum, step_index=step_index, frag_table=frag_table)


def block_terms(x_block, tgt_block, gain, head):
    xf = x_block.astype(jnp.float32)
    ms = lax.optimization_barrier(jnp.mean(xf * xf, axis=-1, keepdims=True))
    normed = (xf * lax.rsqrt(ms + 1e-05) * gain).astype(jnp.bfloat16)
    scale = 1.0 / jnp.sqrt(jnp.float32(D))
    logits = jnp.dot(normed, head, preferred_element_type=jnp.float32) * scale
    expo = jnp.exp(logits)
    total = lax.optimization_barrier(jnp.sum(expo, axis=-1))
    onehot = jnp.arange(V, dtype=jnp.int32)[None, :] == tgt_block[:, None]
    picked = lax.optimization_barrier(jnp.sum(jnp.where(onehot, logits, 0.0), axis=-1))
    loss = jnp.log(total) - picked
    err = (expo / total[:, None] - onehot.astype(jnp.float32)).astype(jnp.bfloat16)
    term = (jnp.dot(normed.T, err, preferred_element_type=jnp.float32) * scale).astype(jnp.bfloat16)
    return (loss, term)

def reference(tokens, targets, norm_gain, weights, anchor, momentum, step_index, frag_table):
    nblocks = TOK_REP // TOK_DEV
    losses = []
    stepped_all = []
    for rep_id in range(REPS):
        head = weights[rep_id].astype(jnp.bfloat16)
        xs = tokens[rep_id].reshape(nblocks, TOK_DEV, D)
        ts = targets[rep_id].reshape(nblocks, TOK_DEV)

        def one(carry, pair):
            loss, term = block_terms(pair[0], pair[1], norm_gain, head)
            return (carry + term.astype(jnp.float32), loss)
        grad, loss = lax.scan(one, jnp.zeros((D, V), jnp.float32), (xs, ts))
        losses.append(loss.reshape(TOK_REP))
        stepped_all.append(weights[rep_id] - 1.0 * grad)
    stepped = jnp.stack(stepped_all)
    pos = step_index[0] % FRAGS
    frag = jnp.sum(jnp.where(jnp.arange(FRAGS, dtype=jnp.int32) == pos, frag_table, 0))
    rows = jnp.arange(D, dtype=jnp.int32)
    chosen = (rows // FRAG_ROWS % FRAGS == frag)[:, None]
    delta = anchor - lax.optimization_barrier(jnp.sum(stepped, axis=0)) / REPS
    new_mom = 0.9 * momentum + delta
    new_w = anchor - 0.7 * (delta + 0.9 * new_mom)
    momentum_out = jnp.where(chosen, new_mom, momentum)
    weights_out = jnp.where(chosen[None], new_w[None], stepped)
    return (jnp.stack(losses), weights_out, momentum_out)
```

```python
import functools

import jax
import jax.numpy as jnp
import numpy as np
from jax import lax
from jax.experimental import pallas as pl
from jax.experimental.pallas import tpu as pltpu
from jax.sharding import PartitionSpec as P

F32 = jnp.float32
BF16 = jnp.bfloat16
MESH = pl.DeviceIdType.MESH

GATHER_ORDER = (0, 2, 6, 1, 4, 3, 7, 5)
SCATTER_ORDER = (5, 7, 3, 4, 1, 6, 2, 0)


def dot(a, b, ca, cb):
    return lax.dot_general(a, b, (((ca,), (cb,)), ((), ())), preferred_element_type=F32)


def kernel(
    tokens, targets, gain, weights, anchor, momentum, step_index, frag_table,
    loss_out, weights_out, momentum_out,
    head, normed_t, grad, logits_t, err_t, tok, rq_half, rq, rx, rp_half, rp, stepped, rows_out, rows_in, new_out, new_in,
    tok_sem, gp_s, gp_r, gx_s, gx_r, gq_s, gq_r, sp_s, sp_r, sx_s, sx_r, sq_s, sq_r, e_s, e_r, n_s, n_r,
):
    rows, vocab = weights.shape
    half = rows // 2
    count, width = tokens.shape[1:]
    frag_count = frag_table.shape[0]
    run = rows // frag_count
    chunk = tok.shape[1]
    scale = np.float32(1.0 / np.sqrt(np.float32(width)))

    r, f = lax.axis_index("rep"), lax.axis_index("fsdp")
    core = r % 2
    z, y, x = f // 8, (f // 2) % 4, f % 2
    p = jnp.where(core == 0, z, y)
    q = jnp.where(core == 0, y, z)

    def device(dp=0, dq=0, dx=0):
        pp, qq, xx = (p + dp) % 4, (q + dq) % 4, (x + dx) % 2
        return (r, jnp.where(core == 0, pp, qq) * 8 + jnp.where(core == 0, qq, pp) * 2 + xx)

    p_up, p_down, q_up, q_down, x_other = device(dp=1), device(dp=3), device(dq=1), device(dq=3), device(dx=1)

    def sibling(j):
        c2, l2 = (core + j) % 2, (r // 2 + j // 2) % 2
        return l2 * 2 + c2

    siblings = [(sibling(j), f) for j in (1, 2, 3)]

    barrier = pltpu.get_barrier_semaphore()
    partners = [p_up, p_down, q_up, q_down, x_other] + siblings
    for partner in partners:
        pl.semaphore_signal(barrier, inc=1, device_id=partner, device_id_type=MESH)

    chunks = count // chunk
    slots = tok.shape[0]

    def token_copy(c):
        return pltpu.make_async_copy(
            tokens.at[0, pl.ds(c * chunk, chunk)], tok.at[c % slots], tok_sem.at[c % slots]
        )

    for c in range(slots):
        token_copy(c).start()
    head[0, pl.ds(0, rows)] = weights[...].astype(BF16)
    pl.semaphore_wait(barrier, len(partners))

    sent = []

    def send(src, dst, s_sem, r_sem, to):
        copy = pltpu.make_async_remote_copy(
            src_ref=src, dst_ref=dst, send_sem=s_sem, recv_sem=r_sem, device_id=to, device_id_type=MESH
        )
        copy.start()
        sent.append(copy)
        return copy

    whole = lambda dq: pl.ds(dq * rows, rows)
    low = lambda dq: pl.ds(dq * rows, half)
    high = lambda dq: pl.ds(dq * rows + half, half)

    def gather_q(i):
        a = send(head.at[i, whole(0)], head.at[i, whole(3)], gq_s.at[i, 0], gq_r.at[i, 0], q_up)
        b = send(head.at[i, whole(0)], head.at[i, whole(1)], gq_s.at[i, 1], gq_r.at[i, 1], q_down)
        return a, b

    def forward_q(i, pair):
        pair[0].wait_recv()
        a = send(head.at[i, low(3)], head.at[i, low(2)], gq_s.at[i, 2], gq_r.at[i, 2], q_up)
        pair[1].wait_recv()
        b = send(head.at[i, high(1)], head.at[i, high(2)], gq_s.at[i, 3], gq_r.at[i, 3], q_down)
        return a, b

    def gather_x(dp):
        return send(head.at[2 * dp, whole(0)], head.at[2 * dp + 1, whole(0)], gx_s.at[dp], gx_r.at[dp], x_other)

    def norm_chunk(c, slot):
        xf = tok[slot].astype(F32)
        inv = lax.rsqrt(jnp.sum(xf * xf, axis=1, keepdims=True) * np.float32(1.0 / width) + np.float32(1e-5))

        def unit(j, carry):
            columns = pl.ds(pl.multiple_of(j * 4 * rows, 128), 4 * rows)
            part = (tok[slot, :, columns].astype(F32) * inv * gain[:, columns]).astype(BF16).T
            for b in range(4):
                bz, by, bx = j // 2, 2 * (j % 2) + b // 2, b % 2
                dp = (jnp.where(core == 0, bz, by) - p + 4) % 4
                dq = (jnp.where(core == 0, by, bz) - q + 4) % 4
                dx = (bx + x) % 2
                normed_t[
                    2 * dp + dx,
                    pl.ds(pl.multiple_of(dq * rows, 16), rows),
                    pl.ds(pl.multiple_of(c * chunk, chunk), chunk),
                ] = part[b * rows : (b + 1) * rows]
            return carry

        lax.fori_loop(0, width // (4 * rows), unit, 0)

    def norm(first, last):
        for c in range(first, last):
            token_copy(c).wait()
            norm_chunk(c, c % slots)
            if c + slots < chunks:
                token_copy(c + slots).start()

    tile = 256

    def add_logits(i, fresh):
        def step(j, carry):
            s = pl.ds(pl.multiple_of(j * tile, tile), tile)
            term = dot(head[i, :, s], normed_t[i], 0, 0)
            if fresh:
                logits_t[s, :] = term
            else:
                logits_t[s, :] += term
            return carry

        lax.fori_loop(0, vocab // tile, step, 0)

    own = head.at[0, whole(0)]
    up = send(own, head.at[6, whole(0)], gp_s.at[0], gp_r.at[0], p_up)
    down = send(own, head.at[2, whole(0)], gp_s.at[1], gp_r.at[1], p_down)
    gx = {0: gather_x(0)}
    gq, fq = {0: gather_q(0)}, {}
    norm(0, 4)
    up.wait_recv()
    up2 = send(head.at[6, low(0)], head.at[4, low(0)], gp_s.at[2], gp_r.at[2], p_up)
    down.wait_recv()
    down2 = send(head.at[2, high(0)], head.at[4, high(0)], gp_s.at[3], gp_r.at[3], p_down)
    gx[1] = gather_x(1)
    gx[3] = gather_x(3)
    gq[2] = gather_q(2)
    gq[6] = gather_q(6)
    gx[0].wait_recv()
    gq[1] = gather_q(1)
    norm(4, 6)
    fq[0] = forward_q(0, gq[0])
    up2.wait_recv()
    down2.wait_recv()
    gx[2] = gather_x(2)
    gq[4] = gather_q(4)
    norm(6, 8)
    fq[2] = forward_q(2, gq[2])
    fq[6] = forward_q(6, gq[6])

    def finish(i, fresh=False):
        fq[i][0].wait_recv()
        fq[i][1].wait_recv()
        add_logits(i, fresh)

    finish(0, True)
    gx[1].wait_recv()
    gq[3] = gather_q(3)
    gx[3].wait_recv()
    gq[7] = gather_q(7)
    fq[1] = forward_q(1, gq[1])
    finish(2)
    gx[2].wait_recv()
    gq[5] = gather_q(5)
    fq[4] = forward_q(4, gq[4])
    finish(6)
    fq[3] = forward_q(3, gq[3])
    finish(1)
    fq[7] = forward_q(7, gq[7])
    finish(4)
    fq[5] = forward_q(5, gq[5])
    finish(3)
    finish(7)
    finish(5)

    lanes = 128

    def soften(j, carry):
        s = pl.ds(pl.multiple_of(j * lanes, lanes), lanes)
        logit = logits_t[:, s] * scale
        expo = jnp.exp(logit)
        total = jnp.sum(expo, axis=0, keepdims=True)
        onehot = lax.broadcasted_iota(jnp.int32, (vocab, lanes), 0) == targets[:, s]
        picked = jnp.sum(jnp.where(onehot, logit, 0.0), axis=0, keepdims=True)
        loss_out[:, s] = jnp.log(total) - picked
        err_t[:, s] = (expo * (1.0 / total) - jnp.where(onehot, 1.0, 0.0)).astype(BF16)
        return carry

    lax.fori_loop(0, count // lanes, soften, 0)

    def term(i, dq):
        grad[i, whole(dq)] = (dot(normed_t[i, whole(dq)], err_t[...], 1, 1) * scale).astype(BF16)

    def start_terms(i):
        term(i, 2)
        a = send(grad.at[i, low(2)], rq_half.at[i, 0], sq_s.at[i, 0], sq_r.at[i, 0], q_up)
        b = send(grad.at[i, high(2)], rq_half.at[i, 1], sq_s.at[i, 1], sq_r.at[i, 1], q_down)
        term(i, 1)
        term(i, 3)
        term(i, 0)
        return a, b

    def add_into(i, where, *others):
        total = grad[i, where].astype(F32)
        for other in others:
            total = total + other[...].astype(F32)
        grad[i, where] = total.astype(BF16)

    def pass_on(i, pair):
        pair[0].wait_recv()
        add_into(i, low(1), rq_half.at[i, 0])
        a = send(grad.at[i, whole(1)], rq.at[i, 0], sq_s.at[i, 2], sq_r.at[i, 2], q_up)
        pair[1].wait_recv()
        add_into(i, high(3), rq_half.at[i, 1])
        b = send(grad.at[i, whole(3)], rq.at[i, 1], sq_s.at[i, 3], sq_r.at[i, 3], q_down)
        return a, b

    halves, wholes, sx = {}, {}, {}
    p_half, p_whole = [], {}

    def settle(i):
        for copy in wholes[i]:
            copy.wait_recv()
        dp, dx = i // 2, i % 2
        if dx:
            add_into(i, whole(0), rq.at[i, 0], rq.at[i, 1])
            sx[dp] = send(grad.at[i, whole(0)], rx.at[dp], sx_s.at[dp], sx_r.at[dp], x_other)
        elif dp == 2:
            sx[2].wait_recv()
            add_into(i, whole(0), rq.at[i, 0], rq.at[i, 1], rx.at[2])
            p_half.append(send(grad.at[i, low(0)], rp_half.at[0], sp_s.at[0], sp_r.at[0], p_up))
            p_half.append(send(grad.at[i, high(0)], rp_half.at[1], sp_s.at[1], sp_r.at[1], p_down))
        elif dp:
            sx[dp].wait_recv()
            add_into(i, whole(0), rq.at[i, 0], rq.at[i, 1], rx.at[dp])
            if dp == 1:
                p_half[0].wait_recv()
                add_into(i, low(0), rp_half.at[0])
                p_whole[0] = send(grad.at[i, whole(0)], rp.at[0], sp_s.at[2], sp_r.at[2], p_up)
            else:
                p_half[1].wait_recv()
                add_into(i, high(0), rp_half.at[1])
                p_whole[1] = send(grad.at[i, whole(0)], rp.at[1], sp_s.at[3], sp_r.at[3], p_down)

    order = SCATTER_ORDER
    halves[order[0]] = start_terms(order[0])
    for k, i in enumerate(order):
        if k + 1 < len(order):
            halves[order[k + 1]] = start_terms(order[k + 1])
        wholes[i] = pass_on(i, halves[i])
        if k:
            settle(order[k - 1])
    for copy in wholes[0]:
        copy.wait_recv()
    sx[0].wait_recv()
    total = grad[0, whole(0)].astype(F32)
    for part in (rq.at[0, 0], rq.at[0, 1], rx.at[0]):
        total = total + part[...].astype(F32)
    for k in (1, 0):
        p_whole[k].wait_recv()
        total = total + rp[k].astype(F32)
    stepped[pl.ds(0, rows)] = weights[...] - total
    stepped[pl.ds(rows, 8)] = jnp.zeros((8, vocab), F32)

    pos = step_index[0] % frag_count
    frag = jnp.int32(0)
    for k in range(frag_count):
        frag = frag + jnp.where(pos == k, frag_table[k], 0)
    pad = rows_out.shape[1]
    part = vocab // 4
    mine = jnp.zeros((pad, vocab), F32)
    for k in range(frag_count):
        mine = jnp.where(frag == k, stepped[pl.ds(k * run, pad)], mine)
    for k in range(4):
        rows_out[k] = mine[:, k * part : (k + 1) * part]
    exchange = [
        send(rows_out.at[to[0]], rows_in.at[j], e_s.at[j], e_r.at[j], to) for j, to in enumerate(siblings)
    ]
    held = jnp.zeros((run, part), F32)
    moment = jnp.zeros((run, part), F32)
    for k in range(frag_count):
        held = jnp.where(frag == k, anchor[pl.ds(k * run, run)], held)
        moment = jnp.where(frag == k, momentum[pl.ds(k * run, run)], moment)
    summed = rows_out[r]
    for j, copy in enumerate(exchange):
        copy.wait_recv()
        summed = summed + rows_in[j]
    delta = held - summed[:run] / 4
    moment = 0.9 * moment + delta
    fresh_rows = held - 0.7 * (delta + 0.9 * moment)
    new_out[pl.ds(0, run)] = fresh_rows
    new_out[pl.ds(run, pad - run)] = jnp.zeros((pad - run, part), F32)
    spread = [send(new_out, new_in.at[j], n_s.at[j], n_r.at[j], to) for j, to in enumerate(siblings)]
    for k in range(frag_count):
        s = pl.ds(k * run, run)
        momentum_out[s] = jnp.where(frag == k, moment, momentum[s])
        weights_out[s, pl.ds(pl.multiple_of(r * part, part), part)] = jnp.where(
            frag == k, fresh_rows, stepped[s, pl.ds(pl.multiple_of(r * part, part), part)]
        )
    for j, copy in enumerate(spread):
        copy.wait_recv()
        columns = pl.ds(pl.multiple_of(siblings[j][0] * part, part), part)
        for k in range(frag_count):
            s = pl.ds(k * run, run)
            weights_out[s, columns] = jnp.where(frag == k, new_in[j, pl.ds(0, run)], stepped[s, columns])
    for copy in sent:
        copy.wait_send()


def on_device(tokens, targets, norm_gain, weights, anchor, momentum, step_index, frag_table):
    _, count, width = tokens.shape
    _, rows, vocab = weights.shape
    half = rows // 2
    part = vocab // 4
    run = rows // frag_table.shape[0]
    pad = -(-run // 8) * 8
    vmem = pl.BlockSpec(memory_space=pltpu.VMEM)
    smem = pl.BlockSpec(memory_space=pltpu.SMEM)
    dma = pltpu.SemaphoreType.DMA
    big = pltpu.VMEM((8, 4 * rows, vocab), BF16)
    loss, weights_out, momentum_out = pl.pallas_call(
        kernel,
        out_shape=(
            jax.ShapeDtypeStruct((1, count), F32),
            jax.ShapeDtypeStruct((rows, vocab), F32),
            jax.ShapeDtypeStruct((rows, part), F32),
        ),
        in_specs=[pl.BlockSpec(memory_space=pl.ANY)] + [vmem] * 5 + [smem] * 2,
        out_specs=(vmem, vmem, vmem),
        scratch_shapes=[
            big,
            pltpu.VMEM((8, 4 * rows, count), BF16),
            big,
            pltpu.VMEM((vocab, count), F32),
            pltpu.VMEM((vocab, count), BF16),
            pltpu.VMEM((4, 128, width), BF16),
            pltpu.VMEM((8, 2, half, vocab), BF16),
            pltpu.VMEM((8, 2, rows, vocab), BF16),
            pltpu.VMEM((4, rows, vocab), BF16),
            pltpu.VMEM((2, half, vocab), BF16),
            pltpu.VMEM((2, rows, vocab), BF16),
            pltpu.VMEM((rows + 8, vocab), F32),
            pltpu.VMEM((4, pad, part), F32),
            pltpu.VMEM((3, pad, part), F32),
            pltpu.VMEM((pad, part), F32),
            pltpu.VMEM((3, pad, part), F32),
            dma((4,)),
            dma((4,)), dma((4,)), dma((4,)), dma((4,)), dma((8, 4)), dma((8, 4)),
            dma((4,)), dma((4,)), dma((4,)), dma((4,)), dma((8, 4)), dma((8, 4)),
            dma((3,)), dma((3,)), dma((3,)), dma((3,)),
        ],
        compiler_params=pltpu.CompilerParams(
            collective_id=0, has_side_effects=True, vmem_limit_bytes=62 * 1024 * 1024
        ),
    )(
        tokens, targets, norm_gain[None], weights[0], anchor, momentum, step_index, frag_table
    )
    return (loss, weights_out[None], momentum_out)


def solution(mesh):
    return jax.shard_map(
        on_device,
        mesh=mesh,
        in_specs=(
            P("rep", "fsdp", None),
            P("rep", "fsdp"),
            P(),
            P("rep", "fsdp", None),
            P("fsdp", "rep"),
            P("fsdp", "rep"),
            P(),
            P(),
        ),
        out_specs=(P("rep", "fsdp"), P("rep", "fsdp", None), P("fsdp", "rep")),
        check_vma=False,
    )
```

```python
import functools

import jax
import jax.numpy as jnp
import numpy as np
from jax import lax
from jax.experimental import pallas as pl
from jax.experimental.pallas import tpu as pltpu
from jax.sharding import PartitionSpec as P

F32 = jnp.float32
BF16 = jnp.bfloat16
MESH = pl.DeviceIdType.MESH

SCATTER_ORDER = (5, 7, 3, 1, 4, 6, 2, 0)
NEAR = 64


def dot(a, b, ca, cb):
    return lax.dot_general(a, b, (((ca,), (cb,)), ((), ())), preferred_element_type=F32)


def kernel(
    tokens, targets, gain, weights, anchor, momentum, step_index, frag_table,
    loss_out, stepped_out, fresh_out, moment_out,
    head, normed_t, grad, logits_t, err_t, tok, rq_half, rq, rx, rx_far, rp_half, rp, stepped, rows_out, rows_in, new_out, new_in,
    tok_sem, gp_s, gp_r, gx_s, gx_r, gf_s, gf_r, gq_s, gq_r,
    sp_s, sp_r, sx_s, sx_r, sf_s, sf_r, sq_s, sq_r, e_s, e_r, n_s, n_r,
):
    rows, vocab = weights.shape
    half = rows // 2
    count, width = tokens.shape[1:]
    frag_count = frag_table.shape[0]
    run = rows // frag_count
    chunk = tok.shape[1]
    scale = np.float32(1.0 / np.sqrt(np.float32(width)))

    r, f = lax.axis_index("rep"), lax.axis_index("fsdp")
    core = r % 2
    z, y, x = f // 8, (f // 2) % 4, f % 2
    p = jnp.where(core == 0, z, y)
    q = jnp.where(core == 0, y, z)

    def device(dp=0, dq=0, dx=0):
        pp, qq, xx = (p + dp) % 4, (q + dq) % 4, (x + dx) % 2
        return (r, jnp.where(core == 0, pp, qq) * 8 + jnp.where(core == 0, qq, pp) * 2 + xx)

    p_up, p_down, q_up, q_down, x_other = device(dp=1), device(dp=3), device(dq=1), device(dq=3), device(dx=1)

    def sibling(j):
        c2, l2 = (core + j) % 2, (r // 2 + j // 2) % 2
        return l2 * 2 + c2

    siblings = [(sibling(j), f) for j in (1, 2, 3)]

    barrier = pltpu.get_barrier_semaphore()
    partners = [p_up, p_down, q_up, q_down, x_other] + siblings
    for partner in partners:
        pl.semaphore_signal(barrier, inc=1, device_id=partner, device_id_type=MESH)

    chunks = count // chunk
    slots = tok.shape[0]

    def token_copy(c):
        return pltpu.make_async_copy(
            tokens.at[0, pl.ds(c * chunk, chunk)], tok.at[c % slots], tok_sem.at[c % slots]
        )

    for c in range(slots):
        token_copy(c).start()
    head[0, pl.ds(0, rows)] = weights[...].astype(BF16)
    pl.semaphore_wait(barrier, len(partners))

    sent = []

    def send(src, dst, s_sem, r_sem, to):
        copy = pltpu.make_async_remote_copy(
            src_ref=src, dst_ref=dst, send_sem=s_sem, recv_sem=r_sem, device_id=to, device_id_type=MESH
        )
        copy.start()
        sent.append(copy)
        return copy

    def whole(dq, i=0):
        return pl.ds(dq * rows, NEAR if i == 5 else rows)

    def low(dq, i=0):
        return pl.ds(dq * rows, NEAR // 2 if i == 5 else half)

    def high(dq, i=0):
        return pl.ds(dq * rows + NEAR // 2, NEAR // 2) if i == 5 else pl.ds(dq * rows + half, half)

    def far(dq):
        return pl.ds(dq * rows + NEAR, rows - NEAR)

    def prefix(i, n):
        return pl.ds(0, n * NEAR // rows if i == 5 else n)

    def gather_q(i):
        a = send(head.at[i, whole(0, i)], head.at[i, whole(3, i)], gq_s.at[i, 0], gq_r.at[i, 0], q_up)
        b = send(head.at[i, whole(0, i)], head.at[i, whole(1, i)], gq_s.at[i, 1], gq_r.at[i, 1], q_down)
        return a, b

    def forward_q(i, pair):
        pair[0].wait_recv()
        a = send(head.at[i, low(3, i)], head.at[i, low(2, i)], gq_s.at[i, 2], gq_r.at[i, 2], q_up)
        pair[1].wait_recv()
        b = send(head.at[i, high(1, i)], head.at[i, high(2, i)], gq_s.at[i, 3], gq_r.at[i, 3], q_down)
        return a, b

    def gather_x(dp):
        i = 2 * dp
        return send(head.at[i, whole(0, i + 1)], head.at[i + 1, whole(0, i + 1)], gx_s.at[dp], gx_r.at[dp], x_other)

    def gather_far(dq):
        return send(head.at[4, far(dq)], head.at[5, far(dq)], gf_s.at[dq], gf_r.at[dq], x_other)

    def norm_chunk(c, slot):
        xf = tok[slot].astype(F32)
        inv = lax.rsqrt(jnp.sum(xf * xf, axis=1, keepdims=True) * np.float32(1.0 / width) + np.float32(1e-5))

        def unit(j, carry):
            columns = pl.ds(pl.multiple_of(j * 4 * rows, 128), 4 * rows)
            part = (tok[slot, :, columns].astype(F32) * inv * gain[:, columns]).astype(BF16).T
            for b in range(4):
                bz, by, bx = j // 2, 2 * (j % 2) + b // 2, b % 2
                dp = (jnp.where(core == 0, bz, by) - p + 4) % 4
                dq = (jnp.where(core == 0, by, bz) - q + 4) % 4
                dx = (bx + x) % 2
                normed_t[
                    2 * dp + dx,
                    pl.ds(pl.multiple_of(dq * rows, 16), rows),
                    pl.ds(pl.multiple_of(c * chunk, chunk), chunk),
                ] = part[b * rows : (b + 1) * rows]
            return carry

        lax.fori_loop(0, width // (4 * rows), unit, 0)

    def norm(first, last):
        for c in range(first, last):
            token_copy(c).wait()
            norm_chunk(c, c % slots)
            if c + slots < chunks:
                token_copy(c + slots).start()

    def add_logits(i, fresh, tile=512):
        if tile == vocab:
            logits_t[...] += dot(head[i], normed_t[i], 0, 0)
            return

        def step(j, carry):
            s = pl.ds(pl.multiple_of(j * tile, tile), tile)
            term = dot(head[i, :, s], normed_t[i], 0, 0)
            if fresh:
                logits_t[s, :] = term
            else:
                logits_t[s, :] += term
            return carry

        lax.fori_loop(0, vocab // tile, step, 0)

    def finish(i, fresh=False, tile=512):
        fq[i][0].wait_recv()
        fq[i][1].wait_recv()
        add_logits(i, fresh, tile)

    own = head.at[0, whole(0)]
    up = send(own, head.at[6, whole(0)], gp_s.at[0], gp_r.at[0], p_up)
    down = send(own, head.at[2, whole(0)], gp_s.at[1], gp_r.at[1], p_down)
    gx, gq, fq, gf = {0: gather_x(0)}, {0: gather_q(0)}, {}, {}
    norm(0, 4)
    up.wait_recv()
    up2 = send(head.at[6, low(0)], head.at[4, low(0)], gp_s.at[2], gp_r.at[2], p_up)
    down.wait_recv()
    down2 = send(head.at[2, high(0)], head.at[4, high(0)], gp_s.at[3], gp_r.at[3], p_down)
    gx[1] = gather_x(1)
    gx[3] = gather_x(3)
    gq[2] = gather_q(2)
    gq[6] = gather_q(6)
    norm(4, 6)
    fq[0] = forward_q(0, gq[0])
    up2.wait_recv()
    down2.wait_recv()
    gq[4] = gather_q(4)
    gx[2] = gather_x(2)
    gf[0] = gather_far(0)
    gx[0].wait_recv()
    gq[1] = gather_q(1)
    norm(6, 8)
    fq[2] = forward_q(2, gq[2])
    fq[6] = forward_q(6, gq[6])
    finish(0, True)
    fq[4] = forward_q(4, gq[4])
    gf[1] = gather_far(1)
    gf[3] = gather_far(3)
    gx[1].wait_recv()
    gq[3] = gather_q(3)
    finish(2)
    fq[4][0].wait_recv()
    fq[4][1].wait_recv()
    gf[2] = gather_far(2)
    gx[3].wait_recv()
    gq[7] = gather_q(7)
    fq[1] = forward_q(1, gq[1])
    finish(6)
    gx[2].wait_recv()
    gq[5] = gather_q(5)
    add_logits(4, False)
    fq[3] = forward_q(3, gq[3])
    finish(1)
    fq[7] = forward_q(7, gq[7])
    fq[5] = forward_q(5, gq[5])
    finish(3)
    for dq in (0, 1, 3, 2):
        gf[dq].wait_recv()
    finish(7)
    finish(5, tile=vocab)

    lanes = 128

    def soften(j, carry):
        s = pl.ds(pl.multiple_of(j * lanes, lanes), lanes)
        logit = logits_t[:, s] * scale
        expo = jnp.exp(logit)
        total = jnp.sum(expo, axis=0, keepdims=True)
        onehot = lax.broadcasted_iota(jnp.int32, (vocab, lanes), 0) == targets[:, s]
        picked = jnp.sum(jnp.where(onehot, logit, 0.0), axis=0, keepdims=True)
        loss_out[:, s] = jnp.log(total) - picked
        err_t[:, s] = (expo * (1.0 / total) - jnp.where(onehot, 1.0, 0.0)).astype(BF16)
        return carry

    lax.fori_loop(0, count // lanes, soften, 0)

    def terms(i, dq):
        two = pl.ds(dq * rows, 2 * rows)
        grad[i, two] = (dot(normed_t[i, two], err_t[...], 1, 1) * scale).astype(BF16)

    def add_into(i, where, *others):
        total = grad[i, where].astype(F32)
        for other in others:
            total = total + other[...].astype(F32)
        grad[i, where] = total.astype(BF16)

    sf = {}

    def take_far(i, *slots_):
        for dq in slots_ if i == 4 else ():
            sf[dq].wait_recv()
            add_into(4, far(dq), rx_far.at[dq])

    def give_far(i, *slots_):
        for dq in slots_ if i == 5 else ():
            sf[dq] = send(grad.at[5, far(dq)], rx_far.at[dq], sf_s.at[dq], sf_r.at[dq], x_other)

    def start_terms(i):
        terms(i, 2)
        take_far(i, 2)
        a = send(grad.at[i, low(2, i)], rq_half.at[i, 0, prefix(i, half)], sq_s.at[i, 0], sq_r.at[i, 0], q_up)
        b = send(grad.at[i, high(2, i)], rq_half.at[i, 1, prefix(i, half)], sq_s.at[i, 1], sq_r.at[i, 1], q_down)
        give_far(i, 2, 3)
        terms(i, 0)
        give_far(i, 1, 0)
        return a, b

    def pass_on(i, pair):
        take_far(i, 1, 3)
        pair[0].wait_recv()
        add_into(i, low(1, i), rq_half.at[i, 0, prefix(i, half)])
        a = send(grad.at[i, whole(1, i)], rq.at[i, 0, prefix(i, rows)], sq_s.at[i, 2], sq_r.at[i, 2], q_up)
        pair[1].wait_recv()
        add_into(i, high(3, i), rq_half.at[i, 1, prefix(i, half)])
        b = send(grad.at[i, whole(3, i)], rq.at[i, 1, prefix(i, rows)], sq_s.at[i, 3], sq_r.at[i, 3], q_down)
        return a, b

    halves, wholes, sx = {}, {}, {}
    p_half, p_whole = [], {}

    def settle(i):
        for copy in wholes[i]:
            copy.wait_recv()
        dp, dx = i // 2, i % 2
        if dx:
            n = prefix(i, rows)
            add_into(i, whole(0, i), rq.at[i, 0, n], rq.at[i, 1, n])
            sx[dp] = send(grad.at[i, whole(0, i)], rx.at[dp, n], sx_s.at[dp], sx_r.at[dp], x_other)
        elif dp == 2:
            take_far(4, 0)
            sx[2].wait_recv()
            add_into(i, whole(0), rq.at[i, 0], rq.at[i, 1])
            add_into(i, whole(0, 5), rx.at[2, prefix(5, rows)])
            p_half.append(send(grad.at[i, low(0)], rp_half.at[0], sp_s.at[0], sp_r.at[0], p_up))
            p_half.append(send(grad.at[i, high(0)], rp_half.at[1], sp_s.at[1], sp_r.at[1], p_down))
        elif dp:
            sx[dp].wait_recv()
            add_into(i, whole(0), rq.at[i, 0], rq.at[i, 1], rx.at[dp])
            if dp == 1:
                p_half[0].wait_recv()
                add_into(i, low(0), rp_half.at[0])
                p_whole[0] = send(grad.at[i, whole(0)], rp.at[0], sp_s.at[2], sp_r.at[2], p_up)
            else:
                p_half[1].wait_recv()
                add_into(i, high(0), rp_half.at[1])
                p_whole[1] = send(grad.at[i, whole(0)], rp.at[1], sp_s.at[3], sp_r.at[3], p_down)

    order = SCATTER_ORDER
    halves[order[0]] = start_terms(order[0])
    for k, i in enumerate(order):
        if k + 1 < len(order):
            halves[order[k + 1]] = start_terms(order[k + 1])
        wholes[i] = pass_on(i, halves[i])
        if k:
            settle(order[k - 1])
    for copy in wholes[0]:
        copy.wait_recv()
    sx[0].wait_recv()
    total = grad[0, whole(0)].astype(F32)
    for part in (rq.at[0, 0], rq.at[0, 1], rx.at[0]):
        total = total + part[...].astype(F32)
    for k in (1, 0):
        p_whole[k].wait_recv()
        total = total + rp[k].astype(F32)
    stepped[pl.ds(0, rows)] = weights[...] - total
    stepped[pl.ds(rows, 8)] = jnp.zeros((8, vocab), F32)

    pos = step_index[0] % frag_count
    frag = jnp.int32(0)
    for k in range(frag_count):
        frag = frag + jnp.where(pos == k, frag_table[k], 0)
    pad = rows_out.shape[1]
    part = vocab // 4
    mine = jnp.zeros((pad, vocab), F32)
    for k in range(frag_count):
        mine = jnp.where(frag == k, stepped[pl.ds(k * run, pad)], mine)
    for k in range(4):
        rows_out[k] = mine[:, k * part : (k + 1) * part]
    exchange = [
        send(rows_out.at[to[0]], rows_in.at[j], e_s.at[j], e_r.at[j], to) for j, to in enumerate(siblings)
    ]
    held = jnp.zeros((run, part), F32)
    moment = jnp.zeros((run, part), F32)
    for k in range(frag_count):
        held = jnp.where(frag == k, anchor[pl.ds(k * run, run)], held)
        moment = jnp.where(frag == k, momentum[pl.ds(k * run, run)], moment)
    summed = rows_out[r]
    for j, copy in enumerate(exchange):
        copy.wait_recv()
        summed = summed + rows_in[j]
    delta = held - summed[:run] / 4
    moment = 0.9 * moment + delta
    moment_out[...] = moment
    fresh_rows = held - 0.7 * (delta + 0.9 * moment)
    new_out[pl.ds(0, run)] = fresh_rows
    new_out[pl.ds(run, pad - run)] = jnp.zeros((pad - run, part), F32)
    spread = [send(new_out, new_in.at[j], n_s.at[j], n_r.at[j], to) for j, to in enumerate(siblings)]
    fresh_out[:, pl.ds(pl.multiple_of(r * part, part), part)] = fresh_rows
    stepped_out[...] = stepped[pl.ds(0, rows)]
    for j, copy in enumerate(spread):
        copy.wait_recv()
        fresh_out[:, pl.ds(pl.multiple_of(siblings[j][0] * part, part), part)] = new_in[j, pl.ds(0, run)]
    for copy in sent:
        copy.wait_send()


def merge(loss, stepped, fresh, moment, momentum, step_index, frag_table, loss_out, weights_out, momentum_out):
    frag_count = frag_table.shape[0]
    run = fresh.shape[0]
    pos = step_index[0] % frag_count
    frag = jnp.int32(0)
    for k in range(frag_count):
        frag = frag + jnp.where(pos == k, frag_table[k], 0)
    loss_out[...] = loss[...]
    for k in range(frag_count):
        s = pl.ds(k * run, run)
        weights_out[s] = jnp.where(frag == k, fresh[...], stepped[s])
        momentum_out[s] = jnp.where(frag == k, moment[...], momentum[s])


def on_device(tokens, targets, norm_gain, weights, anchor, momentum, step_index, frag_table):
    _, count, width = tokens.shape
    _, rows, vocab = weights.shape
    half = rows // 2
    part = vocab // 4
    run = rows // frag_table.shape[0]
    pad = -(-run // 8) * 8
    vmem = pl.BlockSpec(memory_space=pltpu.VMEM)
    smem = pl.BlockSpec(memory_space=pltpu.SMEM)
    dma = pltpu.SemaphoreType.DMA
    big = pltpu.VMEM((8, 4 * rows, vocab), BF16)
    shapes = (
        jax.ShapeDtypeStruct((1, count), F32),
        jax.ShapeDtypeStruct((rows, vocab), F32),
        jax.ShapeDtypeStruct((rows, part), F32),
    )
    loss, stepped, fresh, moment = pl.pallas_call(
        kernel,
        out_shape=shapes[:2] + (jax.ShapeDtypeStruct((run, vocab), F32), jax.ShapeDtypeStruct((run, part), F32)),
        in_specs=[pl.BlockSpec(memory_space=pl.ANY)] + [vmem] * 5 + [smem] * 2,
        out_specs=(vmem,) * 4,
        scratch_shapes=[
            big,
            pltpu.VMEM((8, 4 * rows, count), BF16),
            big,
            pltpu.VMEM((vocab, count), F32),
            pltpu.VMEM((vocab, count), BF16),
            pltpu.VMEM((4, 128, width), BF16),
            pltpu.VMEM((8, 2, half, vocab), BF16),
            pltpu.VMEM((8, 2, rows, vocab), BF16),
            pltpu.VMEM((4, rows, vocab), BF16),
            pltpu.VMEM((4, rows - NEAR, vocab), BF16),
            pltpu.VMEM((2, half, vocab), BF16),
            pltpu.VMEM((2, rows, vocab), BF16),
            pltpu.VMEM((rows + 8, vocab), F32),
            pltpu.VMEM((4, pad, part), F32),
            pltpu.VMEM((3, pad, part), F32),
            pltpu.VMEM((pad, part), F32),
            pltpu.VMEM((3, pad, part), F32),
            dma((4,)),
            dma((4,)), dma((4,)), dma((4,)), dma((4,)), dma((4,)), dma((4,)), dma((8, 4)), dma((8, 4)),
            dma((4,)), dma((4,)), dma((4,)), dma((4,)), dma((4,)), dma((4,)), dma((8, 4)), dma((8, 4)),
            dma((3,)), dma((3,)), dma((3,)), dma((3,)),
        ],
        compiler_params=pltpu.CompilerParams(
            collective_id=0, has_side_effects=True, vmem_limit_bytes=62 * 1024 * 1024
        ),
    )(
        tokens, targets, norm_gain[None], weights[0], anchor, momentum, step_index, frag_table
    )
    loss, weights_out, momentum_out = pl.pallas_call(
        merge, out_shape=shapes, in_specs=[vmem] * 5 + [smem] * 2, out_specs=(vmem,) * 3
    )(loss, stepped, fresh, moment, momentum, step_index, frag_table)
    return (loss, weights_out[None], momentum_out)


def solution(mesh):
    return jax.shard_map(
        on_device,
        mesh=mesh,
        in_specs=(
            P("rep", "fsdp", None),
            P("rep", "fsdp"),
            P(),
            P("rep", "fsdp", None),
            P("fsdp", "rep"),
            P("fsdp", "rep"),
            P(),
            P(),
        ),
        out_specs=(P("rep", "fsdp"), P("rep", "fsdp", None), P("fsdp", "rep")),
        check_vma=False,
    )
```

```python
import functools

import jax
import jax.numpy as jnp
import numpy as np
from jax import lax
from jax.experimental import pallas as pl
from jax.experimental.pallas import tpu as pltpu
from jax.sharding import PartitionSpec as P

F32 = jnp.float32
BF16 = jnp.bfloat16
MESH = pl.DeviceIdType.MESH

SCATTER_ORDER = (5, 7, 3, 1, 4, 6, 2, 0)
SLOT = (0, 1, 3, 2)
NEAR = 64


def dot(a, b, ca, cb):
    return lax.dot_general(a, b, (((ca,), (cb,)), ((), ())), preferred_element_type=F32)


def kernel(
    tokens, targets, gain, weights, anchor, momentum, step_index, frag_table,
    loss_out, stepped_out, fresh_out, moment_out,
    head, normed_t, grad, logits_t, err_t, tok, rq_half, rq, rx, rx_far, rp_half, rp, stepped, rows_out, rows_in, new_out, new_in,
    tok_sem, gp_s, gp_r, gx_s, gx_r, gf_s, gf_r, gq_s, gq_r,
    sp_s, sp_r, sx_s, sx_r, sf_s, sf_r, sq_s, sq_r, e_s, e_r, n_s, n_r,
):
    rows, vocab = weights.shape
    half = rows // 2
    count, width = tokens.shape[1:]
    frag_count = frag_table.shape[0]
    run = rows // frag_count
    chunk = tok.shape[1]
    scale = np.float32(1.0 / np.sqrt(np.float32(width)))

    r, f = lax.axis_index("rep"), lax.axis_index("fsdp")
    core = r % 2
    z, y, x = f // 8, (f // 2) % 4, f % 2
    p = jnp.where(core == 0, z, y)
    q = jnp.where(core == 0, y, z)

    def device(dp=0, dq=0, dx=0):
        pp, qq, xx = (p + dp) % 4, (q + dq) % 4, (x + dx) % 2
        return (r, jnp.where(core == 0, pp, qq) * 8 + jnp.where(core == 0, qq, pp) * 2 + xx)

    p_up, p_down, q_up, q_down, x_other = device(dp=1), device(dp=3), device(dq=1), device(dq=3), device(dx=1)

    def sibling(j):
        c2, l2 = (core + j) % 2, (r // 2 + j // 2) % 2
        return l2 * 2 + c2

    siblings = [(sibling(j), f) for j in (1, 2, 3)]

    barrier = pltpu.get_barrier_semaphore()
    partners = [p_up, p_down, q_up, q_down, x_other] + siblings
    for partner in partners:
        pl.semaphore_signal(barrier, inc=1, device_id=partner, device_id_type=MESH)

    chunks = count // chunk
    slots = tok.shape[0]

    def token_copy(c):
        return pltpu.make_async_copy(
            tokens.at[0, pl.ds(c * chunk, chunk)], tok.at[c % slots], tok_sem.at[c % slots]
        )

    for c in range(slots):
        token_copy(c).start()
    head[0, pl.ds(0, rows)] = weights[...].astype(BF16)
    pl.semaphore_wait(barrier, len(partners))

    sent = []

    def send(src, dst, s_sem, r_sem, to):
        copy = pltpu.make_async_remote_copy(
            src_ref=src, dst_ref=dst, send_sem=s_sem, recv_sem=r_sem, device_id=to, device_id_type=MESH
        )
        copy.start()
        sent.append(copy)
        return copy

    def whole(dq, i=0):
        return pl.ds(SLOT[dq] * rows, NEAR if i == 5 else rows)

    def low(dq, i=0):
        return pl.ds(SLOT[dq] * rows, NEAR // 2 if i == 5 else half)

    def high(dq, i=0):
        cut = NEAR // 2 if i == 5 else half
        return pl.ds(SLOT[dq] * rows + cut, cut)

    def far(dq):
        return pl.ds(SLOT[dq] * rows + NEAR, rows - NEAR)

    def prefix(i, n):
        return pl.ds(0, n * NEAR // rows if i == 5 else n)

    def gather_q(i):
        a = send(head.at[i, whole(0, i)], head.at[i, whole(3, i)], gq_s.at[i, 0], gq_r.at[i, 0], q_up)
        b = send(head.at[i, whole(0, i)], head.at[i, whole(1, i)], gq_s.at[i, 1], gq_r.at[i, 1], q_down)
        return a, b

    def forward_q(i, pair):
        pair[0].wait_recv()
        a = send(head.at[i, low(3, i)], head.at[i, low(2, i)], gq_s.at[i, 2], gq_r.at[i, 2], q_up)
        pair[1].wait_recv()
        b = send(head.at[i, high(1, i)], head.at[i, high(2, i)], gq_s.at[i, 3], gq_r.at[i, 3], q_down)
        return a, b

    def gather_x(dp):
        i = 2 * dp
        return send(head.at[i, whole(0, i + 1)], head.at[i + 1, whole(0, i + 1)], gx_s.at[dp], gx_r.at[dp], x_other)

    def gather_far(dq):
        return send(head.at[4, far(dq)], head.at[5, far(dq)], gf_s.at[dq], gf_r.at[dq], x_other)

    def norm_chunk(c, slot):
        xf = tok[slot].astype(F32)
        inv = lax.rsqrt(jnp.sum(xf * xf, axis=1, keepdims=True) * np.float32(1.0 / width) + np.float32(1e-5))

        def unit(j, carry):
            columns = pl.ds(pl.multiple_of(j * 4 * rows, 128), 4 * rows)
            part = (tok[slot, :, columns].astype(F32) * inv * gain[:, columns]).astype(BF16).T
            for b in range(4):
                bz, by, bx = j // 2, 2 * (j % 2) + b // 2, b % 2
                dp = (jnp.where(core == 0, bz, by) - p + 4) % 4
                dq = (jnp.where(core == 0, by, bz) - q + 4) % 4
                dx = (bx + x) % 2
                normed_t[
                    2 * dp + dx,
                    pl.ds(pl.multiple_of((dq ^ (dq >> 1)) * rows, 16), rows),
                    pl.ds(pl.multiple_of(c * chunk, chunk), chunk),
                ] = part[b * rows : (b + 1) * rows]
            return carry

        lax.fori_loop(0, width // (4 * rows), unit, 0)

    def norm(first, last):
        for c in range(first, last):
            token_copy(c).wait()
            norm_chunk(c, c % slots)
            if c + slots < chunks:
                token_copy(c + slots).start()

    early = pl.ds(0, 3 * rows)
    last = pl.ds(3 * rows, rows)

    def add_logits(i, where=pl.ds(0, 4 * rows), fresh=False):
        tile = vocab // 2

        def step(j, carry):
            s = pl.ds(pl.multiple_of(j * tile, tile), tile)
            term = dot(head[i, where, s], normed_t[i, where], 0, 0)
            if fresh:
                logits_t[s, :] = term
            else:
                logits_t[s, :] += term
            return carry

        lax.fori_loop(0, vocab // tile, step, 0)

    def settle_q(i):
        fq[i][0].wait_recv()
        fq[i][1].wait_recv()

    def finish(i, fresh=False):
        settle_q(i)
        add_logits(i, fresh=fresh)

    own = head.at[0, whole(0)]
    up = send(own, head.at[6, whole(0)], gp_s.at[0], gp_r.at[0], p_up)
    down = send(own, head.at[2, whole(0)], gp_s.at[1], gp_r.at[1], p_down)
    gx, gq, fq, gf = {0: gather_x(0)}, {0: gather_q(0)}, {}, {}
    norm(0, 4)
    up.wait_recv()
    up2 = send(head.at[6, low(0)], head.at[4, low(0)], gp_s.at[2], gp_r.at[2], p_up)
    down.wait_recv()
    down2 = send(head.at[2, high(0)], head.at[4, high(0)], gp_s.at[3], gp_r.at[3], p_down)
    gx[1] = gather_x(1)
    gx[3] = gather_x(3)
    gq[2] = gather_q(2)
    gq[6] = gather_q(6)
    norm(4, 6)
    fq[0] = forward_q(0, gq[0])
    up2.wait_recv()
    down2.wait_recv()
    gq[4] = gather_q(4)
    gx[2] = gather_x(2)
    gf[0] = gather_far(0)
    gx[0].wait_recv()
    gq[1] = gather_q(1)
    norm(6, 8)
    fq[2] = forward_q(2, gq[2])
    fq[6] = forward_q(6, gq[6])
    finish(0, fresh=True)
    fq[4] = forward_q(4, gq[4])
    gf[1] = gather_far(1)
    gf[3] = gather_far(3)
    gx[1].wait_recv()
    gq[3] = gather_q(3)
    finish(2)
    fq[4][0].wait_recv()
    fq[4][1].wait_recv()
    gf[2] = gather_far(2)
    gx[3].wait_recv()
    gq[7] = gather_q(7)
    fq[1] = forward_q(1, gq[1])
    finish(6)
    gx[2].wait_recv()
    gq[5] = gather_q(5)
    fq[3] = forward_q(3, gq[3])
    add_logits(4)
    fq[7] = forward_q(7, gq[7])
    finish(1)
    fq[5] = forward_q(5, gq[5])
    add_logits(3, early)
    add_logits(7, early)
    for dq in (0, 1, 3):
        gf[dq].wait_recv()
    add_logits(5, early)
    gf[2].wait_recv()
    tail = (3, 7, 5)
    for i in tail:
        settle_q(i)
    logits_t[...] += dot(
        jnp.concatenate([head[i, last] for i in tail]), jnp.concatenate([normed_t[i, last] for i in tail]), 0, 0
    )

    lanes = 128

    def soften(j, carry):
        s = pl.ds(pl.multiple_of(j * lanes, lanes), lanes)
        logit = logits_t[:, s] * scale
        expo = jnp.exp(logit)
        total = jnp.sum(expo, axis=0, keepdims=True)
        onehot = lax.broadcasted_iota(jnp.int32, (vocab, lanes), 0) == targets[:, s]
        picked = jnp.sum(jnp.where(onehot, logit, 0.0), axis=0, keepdims=True)
        loss_out[:, s] = jnp.log(total) - picked
        err_t[:, s] = (expo * (1.0 / total) - jnp.where(onehot, 1.0, 0.0)).astype(BF16)
        return carry

    lax.fori_loop(0, count // lanes, soften, 0)

    def terms(i, slot):
        two = pl.ds(slot * rows, 2 * rows)
        grad[i, two] = (dot(normed_t[i, two], err_t[...], 1, 1) * scale).astype(BF16)

    def add_into(i, where, *others):
        total = grad[i, where].astype(F32)
        for other in others:
            total = total + other[...].astype(F32)
        grad[i, where] = total.astype(BF16)

    sf = {}

    def take_far(i, *slots_):
        for dq in slots_ if i == 4 else ():
            sf[dq].wait_recv()
            add_into(4, far(dq), rx_far.at[dq])

    def give_far(i, *slots_):
        for dq in slots_ if i == 5 else ():
            sf[dq] = send(grad.at[5, far(dq)], rx_far.at[dq], sf_s.at[dq], sf_r.at[dq], x_other)

    def start_terms(i):
        terms(i, 2)
        take_far(i, 2)
        a = send(grad.at[i, low(2, i)], rq_half.at[i, 0, prefix(i, half)], sq_s.at[i, 0], sq_r.at[i, 0], q_up)
        b = send(grad.at[i, high(2, i)], rq_half.at[i, 1, prefix(i, half)], sq_s.at[i, 1], sq_r.at[i, 1], q_down)
        give_far(i, 2, 3)
        terms(i, 0)
        give_far(i, 1, 0)
        return a, b

    def pass_on(i, pair):
        take_far(i, 1, 3)
        pair[0].wait_recv()
        add_into(i, low(1, i), rq_half.at[i, 0, prefix(i, half)])
        a = send(grad.at[i, whole(1, i)], rq.at[i, 0, prefix(i, rows)], sq_s.at[i, 2], sq_r.at[i, 2], q_up)
        pair[1].wait_recv()
        add_into(i, high(3, i), rq_half.at[i, 1, prefix(i, half)])
        b = send(grad.at[i, whole(3, i)], rq.at[i, 1, prefix(i, rows)], sq_s.at[i, 3], sq_r.at[i, 3], q_down)
        return a, b

    halves, wholes, sx = {}, {}, {}
    p_half, p_whole = [], {}

    def settle(i):
        for copy in wholes[i]:
            copy.wait_recv()
        dp, dx = i // 2, i % 2
        if dx:
            n = prefix(i, rows)
            add_into(i, whole(0, i), rq.at[i, 0, n], rq.at[i, 1, n])
            sx[dp] = send(grad.at[i, whole(0, i)], rx.at[dp, n], sx_s.at[dp], sx_r.at[dp], x_other)
        elif dp == 2:
            take_far(4, 0)
            sx[2].wait_recv()
            add_into(i, whole(0), rq.at[i, 0], rq.at[i, 1])
            add_into(i, whole(0, 5), rx.at[2, prefix(5, rows)])
            p_half.append(send(grad.at[i, low(0)], rp_half.at[0], sp_s.at[0], sp_r.at[0], p_up))
            p_half.append(send(grad.at[i, high(0)], rp_half.at[1], sp_s.at[1], sp_r.at[1], p_down))
        elif dp:
            sx[dp].wait_recv()
            add_into(i, whole(0), rq.at[i, 0], rq.at[i, 1], rx.at[dp])
            if dp == 1:
                p_half[0].wait_recv()
                add_into(i, low(0), rp_half.at[0])
                p_whole[0] = send(grad.at[i, whole(0)], rp.at[0], sp_s.at[2], sp_r.at[2], p_up)
            else:
                p_half[1].wait_recv()
                add_into(i, high(0), rp_half.at[1])
                p_whole[1] = send(grad.at[i, whole(0)], rp.at[1], sp_s.at[3], sp_r.at[3], p_down)

    order = SCATTER_ORDER
    halves[order[0]] = start_terms(order[0])
    for k, i in enumerate(order):
        if k + 1 < len(order):
            halves[order[k + 1]] = start_terms(order[k + 1])
        wholes[i] = pass_on(i, halves[i])
        if k:
            settle(order[k - 1])
    for copy in wholes[0]:
        copy.wait_recv()
    sx[0].wait_recv()
    total = grad[0, whole(0)].astype(F32)
    for part in (rq.at[0, 0], rq.at[0, 1], rx.at[0]):
        total = total + part[...].astype(F32)
    for k in (1, 0):
        p_whole[k].wait_recv()
        total = total + rp[k].astype(F32)
    stepped[pl.ds(0, rows)] = weights[...] - total
    stepped[pl.ds(rows, 8)] = jnp.zeros((8, vocab), F32)

    pos = step_index[0] % frag_count
    frag = jnp.int32(0)
    for k in range(frag_count):
        frag = frag + jnp.where(pos == k, frag_table[k], 0)
    pad = rows_out.shape[1]
    part = vocab // 4
    mine = jnp.zeros((pad, vocab), F32)
    for k in range(frag_count):
        mine = jnp.where(frag == k, stepped[pl.ds(k * run, pad)], mine)
    for k in range(4):
        rows_out[k] = mine[:, k * part : (k + 1) * part]
    exchange = [
        send(rows_out.at[to[0]], rows_in.at[j], e_s.at[j], e_r.at[j], to) for j, to in enumerate(siblings)
    ]
    held = jnp.zeros((run, part), F32)
    moment = jnp.zeros((run, part), F32)
    for k in range(frag_count):
        held = jnp.where(frag == k, anchor[pl.ds(k * run, run)], held)
        moment = jnp.where(frag == k, momentum[pl.ds(k * run, run)], moment)
    summed = rows_out[r]
    for j, copy in enumerate(exchange):
        copy.wait_recv()
        summed = summed + rows_in[j]
    delta = held - summed[:run] / 4
    moment = 0.9 * moment + delta
    moment_out[...] = moment
    fresh_rows = held - 0.7 * (delta + 0.9 * moment)
    new_out[pl.ds(0, run)] = fresh_rows
    new_out[pl.ds(run, pad - run)] = jnp.zeros((pad - run, part), F32)
    spread = [send(new_out, new_in.at[j], n_s.at[j], n_r.at[j], to) for j, to in enumerate(siblings)]
    fresh_out[:, pl.ds(pl.multiple_of(r * part, part), part)] = fresh_rows
    stepped_out[...] = stepped[pl.ds(0, rows)]
    for j, copy in enumerate(spread):
        copy.wait_recv()
        fresh_out[:, pl.ds(pl.multiple_of(siblings[j][0] * part, part), part)] = new_in[j, pl.ds(0, run)]
    for copy in sent:
        copy.wait_send()


def merge(loss, stepped, fresh, moment, momentum, step_index, frag_table, loss_out, weights_out, momentum_out):
    frag_count = frag_table.shape[0]
    run = fresh.shape[0]
    pos = step_index[0] % frag_count
    frag = jnp.int32(0)
    for k in range(frag_count):
        frag = frag + jnp.where(pos == k, frag_table[k], 0)
    loss_out[...] = loss[...]
    for k in range(frag_count):
        s = pl.ds(k * run, run)
        weights_out[s] = jnp.where(frag == k, fresh[...], stepped[s])
        momentum_out[s] = jnp.where(frag == k, moment[...], momentum[s])


def on_device(tokens, targets, norm_gain, weights, anchor, momentum, step_index, frag_table):
    _, count, width = tokens.shape
    _, rows, vocab = weights.shape
    half = rows // 2
    part = vocab // 4
    run = rows // frag_table.shape[0]
    pad = -(-run // 8) * 8
    vmem = pl.BlockSpec(memory_space=pltpu.VMEM)
    smem = pl.BlockSpec(memory_space=pltpu.SMEM)
    dma = pltpu.SemaphoreType.DMA
    big = pltpu.VMEM((8, 4 * rows, vocab), BF16)
    shapes = (
        jax.ShapeDtypeStruct((1, count), F32),
        jax.ShapeDtypeStruct((rows, vocab), F32),
        jax.ShapeDtypeStruct((rows, part), F32),
    )
    loss, stepped, fresh, moment = pl.pallas_call(
        kernel,
        out_shape=shapes[:2] + (jax.ShapeDtypeStruct((run, vocab), F32), jax.ShapeDtypeStruct((run, part), F32)),
        in_specs=[pl.BlockSpec(memory_space=pl.ANY)] + [vmem] * 5 + [smem] * 2,
        out_specs=(vmem,) * 4,
        scratch_shapes=[
            big,
            pltpu.VMEM((8, 4 * rows, count), BF16),
            big,
            pltpu.VMEM((vocab, count), F32),
            pltpu.VMEM((vocab, count), BF16),
            pltpu.VMEM((4, 128, width), BF16),
            pltpu.VMEM((8, 2, half, vocab), BF16),
            pltpu.VMEM((8, 2, rows, vocab), BF16),
            pltpu.VMEM((4, rows, vocab), BF16),
            pltpu.VMEM((4, rows - NEAR, vocab), BF16),
            pltpu.VMEM((2, half, vocab), BF16),
            pltpu.VMEM((2, rows, vocab), BF16),
            pltpu.VMEM((rows + 8, vocab), F32),
            pltpu.VMEM((4, pad, part), F32),
            pltpu.VMEM((3, pad, part), F32),
            pltpu.VMEM((pad, part), F32),
            pltpu.VMEM((3, pad, part), F32),
            dma((4,)),
            dma((4,)), dma((4,)), dma((4,)), dma((4,)), dma((4,)), dma((4,)), dma((8, 4)), dma((8, 4)),
            dma((4,)), dma((4,)), dma((4,)), dma((4,)), dma((4,)), dma((4,)), dma((8, 4)), dma((8, 4)),
            dma((3,)), dma((3,)), dma((3,)), dma((3,)),
        ],
        compiler_params=pltpu.CompilerParams(
            collective_id=0, has_side_effects=True, vmem_limit_bytes=62 * 1024 * 1024
        ),
    )(
        tokens, targets, norm_gain[None], weights[0], anchor, momentum, step_index, frag_table
    )
    loss, weights_out, momentum_out = pl.pallas_call(
        merge, out_shape=shapes, in_specs=[vmem] * 5 + [smem] * 2, out_specs=(vmem,) * 3
    )(loss, stepped, fresh, moment, momentum, step_index, frag_table)
    return (loss, weights_out[None], momentum_out)


def solution(mesh):
    return jax.shard_map(
        on_device,
        mesh=mesh,
        in_specs=(
            P("rep", "fsdp", None),
            P("rep", "fsdp"),
            P(),
            P("rep", "fsdp", None),
            P("fsdp", "rep"),
            P("fsdp", "rep"),
            P(),
            P(),
        ),
        out_specs=(P("rep", "fsdp"), P("rep", "fsdp", None), P("fsdp", "rep")),
        check_vma=False,
    )
```

```python
import functools

import jax
import jax.numpy as jnp
import numpy as np
from jax import lax
from jax.experimental import pallas as pl
from jax.experimental.pallas import tpu as pltpu
from jax.sharding import PartitionSpec as P

F32 = jnp.float32
BF16 = jnp.bfloat16
MESH = pl.DeviceIdType.MESH

SCATTER_ORDER = (5, 7, 3, 1, 4, 6, 2, 0)
FIRST = 32
ROLL = (16, 40, 80)
SLOT = (0, 1, 3, 2)
NEAR = 64


def dot(a, b, ca, cb):
    return lax.dot_general(a, b, (((ca,), (cb,)), ((), ())), preferred_element_type=F32)


def kernel(
    tokens, targets, gain, weights, anchor, momentum, step_index, frag_table,
    loss_out, stepped_out, fresh_out, moment_out,
    head, normed_t, grad, logits_t, err_t, tok, rq_half, rq, rx, rx_far, rp_half, rp, rolled, rows_out, rows_in, new_out, new_in,
    tok_sem, gp_s, gp_r, gx_s, gx_r, gf_s, gf_r, gq_s, gq_r,
    sp_s, sp_r, sx_s, sx_r, sf_s, sf_r, sq_s, sq_r, e_s, e_r, n_s, n_r,
):
    rows, vocab = weights.shape
    half = rows // 2
    count, width = tokens.shape[1:]
    frag_count = frag_table.shape[0]
    run = rows // frag_count
    chunk = tok.shape[1]
    scale = np.float32(1.0 / np.sqrt(np.float32(width)))

    r, f = lax.axis_index("rep"), lax.axis_index("fsdp")
    core = r % 2
    z, y, x = f // 8, (f // 2) % 4, f % 2
    p = jnp.where(core == 0, z, y)
    q = jnp.where(core == 0, y, z)

    def device(dp=0, dq=0, dx=0):
        pp, qq, xx = (p + dp) % 4, (q + dq) % 4, (x + dx) % 2
        return (r, jnp.where(core == 0, pp, qq) * 8 + jnp.where(core == 0, qq, pp) * 2 + xx)

    p_up, p_down, q_up, q_down, x_other = device(dp=1), device(dp=3), device(dq=1), device(dq=3), device(dx=1)

    def sibling(j):
        c2, l2 = (core + j) % 2, (r // 2 + j // 2) % 2
        return l2 * 2 + c2

    siblings = [(sibling(j), f) for j in (1, 2, 3)]

    barrier = pltpu.get_barrier_semaphore()
    partners = [p_up, p_down, q_up, q_down, x_other] + siblings
    for partner in partners:
        pl.semaphore_signal(barrier, inc=1, device_id=partner, device_id_type=MESH)

    chunks = count // chunk
    slots = tok.shape[0]

    def token_copy(c):
        return pltpu.make_async_copy(
            tokens.at[0, pl.ds(c * chunk, chunk)], tok.at[c % slots], tok_sem.at[c % slots]
        )

    for c in range(slots):
        token_copy(c).start()
    pos = step_index[0] % frag_count
    frag = jnp.int32(0)
    for k in range(frag_count):
        frag = frag + jnp.where(pos == k, frag_table[k], 0)
    bits = [frag % 2 == 1, frag // 2 % 2 == 1, frag // 4 == 1]

    def roll_up(value):
        for bit, step in zip(bits, ROLL):
            value = jnp.where(bit, jnp.concatenate([value[step:], value[:step]]), value)
        return value

    rolled[...] = roll_up(weights[...])
    head[0, pl.ds(0, rows)] = rolled[...].astype(BF16)
    pl.semaphore_wait(barrier, len(partners))

    sent = []

    def send(src, dst, s_sem, r_sem, to):
        copy = pltpu.make_async_remote_copy(
            src_ref=src, dst_ref=dst, send_sem=s_sem, recv_sem=r_sem, device_id=to, device_id_type=MESH
        )
        copy.start()
        sent.append(copy)
        return copy

    def whole(dq, i=0):
        return pl.ds(SLOT[dq] * rows, NEAR if i == 5 else rows)

    def low(dq, i=0):
        return pl.ds(SLOT[dq] * rows, NEAR // 2 if i == 5 else half)

    def high(dq, i=0):
        cut = NEAR // 2 if i == 5 else half
        return pl.ds(SLOT[dq] * rows + cut, cut)

    def far(dq):
        return pl.ds(SLOT[dq] * rows + NEAR, rows - NEAR)

    def gather_q(i):
        a = send(head.at[i, whole(0, i)], head.at[i, whole(3, i)], gq_s.at[i, 0], gq_r.at[i, 0], q_up)
        b = send(head.at[i, whole(0, i)], head.at[i, whole(1, i)], gq_s.at[i, 1], gq_r.at[i, 1], q_down)
        return a, b

    def forward_q(i, pair):
        pair[0].wait_recv()
        a = send(head.at[i, low(3, i)], head.at[i, low(2, i)], gq_s.at[i, 2], gq_r.at[i, 2], q_up)
        pair[1].wait_recv()
        b = send(head.at[i, high(1, i)], head.at[i, high(2, i)], gq_s.at[i, 3], gq_r.at[i, 3], q_down)
        return a, b

    def gather_x(dp):
        i = 2 * dp
        return send(head.at[i, whole(0, i + 1)], head.at[i + 1, whole(0, i + 1)], gx_s.at[dp], gx_r.at[dp], x_other)

    def gather_far(dq):
        return send(head.at[4, far(dq)], head.at[5, far(dq)], gf_s.at[dq], gf_r.at[dq], x_other)

    def norm_chunk(c, slot):
        xf = tok[slot].astype(F32)
        inv = lax.rsqrt(jnp.sum(xf * xf, axis=1, keepdims=True) * np.float32(1.0 / width) + np.float32(1e-5))

        def unit(j, carry):
            columns = pl.ds(pl.multiple_of(j * 4 * rows, 128), 4 * rows)
            part = (tok[slot, :, columns].astype(F32) * inv * gain[:, columns]).T
            for b in range(4):
                bz, by, bx = j // 2, 2 * (j % 2) + b // 2, b % 2
                dp = (jnp.where(core == 0, bz, by) - p + 4) % 4
                dq = (jnp.where(core == 0, by, bz) - q + 4) % 4
                dx = (bx + x) % 2
                normed_t[
                    2 * dp + dx,
                    pl.ds(pl.multiple_of((dq ^ (dq >> 1)) * rows, 16), rows),
                    pl.ds(pl.multiple_of(c * chunk, chunk), chunk),
                ] = roll_up(part[b * rows : (b + 1) * rows]).astype(BF16)
            return carry

        lax.fori_loop(0, width // (4 * rows), unit, 0)

    def norm(first, last):
        for c in range(first, last):
            token_copy(c).wait()
            norm_chunk(c, c % slots)
            if c + slots < chunks:
                token_copy(c + slots).start()

    early = pl.ds(0, 3 * rows)
    last = pl.ds(3 * rows, rows)

    def add_logits(i, where=pl.ds(0, 4 * rows), fresh=False):
        tile = vocab // 2

        def step(j, carry):
            s = pl.ds(pl.multiple_of(j * tile, tile), tile)
            term = dot(head[i, where, s], normed_t[i, where], 0, 0)
            if fresh:
                logits_t[s, :] = term
            else:
                logits_t[s, :] += term
            return carry

        lax.fori_loop(0, vocab // tile, step, 0)

    def settle_q(i):
        fq[i][0].wait_recv()
        fq[i][1].wait_recv()

    def finish(i, fresh=False):
        settle_q(i)
        add_logits(i, fresh=fresh)

    own = head.at[0, whole(0)]
    up = send(own, head.at[6, whole(0)], gp_s.at[0], gp_r.at[0], p_up)
    down = send(own, head.at[2, whole(0)], gp_s.at[1], gp_r.at[1], p_down)
    gx, gq, fq, gf = {0: gather_x(0)}, {0: gather_q(0)}, {}, {}
    norm(0, 4)
    up.wait_recv()
    up2 = send(head.at[6, low(0)], head.at[4, low(0)], gp_s.at[2], gp_r.at[2], p_up)
    down.wait_recv()
    down2 = send(head.at[2, high(0)], head.at[4, high(0)], gp_s.at[3], gp_r.at[3], p_down)
    gx[1] = gather_x(1)
    gx[3] = gather_x(3)
    gq[2] = gather_q(2)
    gq[6] = gather_q(6)
    norm(4, 6)
    fq[0] = forward_q(0, gq[0])
    up2.wait_recv()
    down2.wait_recv()
    gq[4] = gather_q(4)
    gx[2] = gather_x(2)
    gf[0] = gather_far(0)
    gx[0].wait_recv()
    gq[1] = gather_q(1)
    norm(6, 8)
    fq[2] = forward_q(2, gq[2])
    fq[6] = forward_q(6, gq[6])
    finish(0, fresh=True)
    fq[4] = forward_q(4, gq[4])
    gf[1] = gather_far(1)
    gf[3] = gather_far(3)
    gx[1].wait_recv()
    gq[3] = gather_q(3)
    finish(2)
    fq[4][0].wait_recv()
    fq[4][1].wait_recv()
    gf[2] = gather_far(2)
    gx[3].wait_recv()
    gq[7] = gather_q(7)
    fq[1] = forward_q(1, gq[1])
    finish(6)
    gx[2].wait_recv()
    gq[5] = gather_q(5)
    fq[3] = forward_q(3, gq[3])
    add_logits(4)
    fq[7] = forward_q(7, gq[7])
    finish(1)
    fq[5] = forward_q(5, gq[5])
    add_logits(3, early)
    add_logits(7, early)
    for dq in (0, 1, 3):
        gf[dq].wait_recv()
    add_logits(5, early)
    gf[2].wait_recv()
    tail = (3, 7, 5)
    for i in tail:
        settle_q(i)
    logits_t[...] += dot(
        jnp.concatenate([head[i, last] for i in tail]), jnp.concatenate([normed_t[i, last] for i in tail]), 0, 0
    )

    lanes = 128

    def soften(j, carry):
        s = pl.ds(pl.multiple_of(j * lanes, lanes), lanes)
        logit = logits_t[:, s] * scale
        expo = jnp.exp(logit)
        total = jnp.sum(expo, axis=0, keepdims=True)
        onehot = lax.broadcasted_iota(jnp.int32, (vocab, lanes), 0) == targets[:, s]
        picked = jnp.sum(jnp.where(onehot, logit, 0.0), axis=0, keepdims=True)
        loss_out[:, s] = jnp.log(total) - picked
        err_t[:, s] = (expo * (1.0 / total) - jnp.where(onehot, 1.0, 0.0)).astype(BF16)
        return carry

    lax.fori_loop(0, count // lanes, soften, 0)

    def terms(i, slot):
        two = pl.ds(slot * rows, 2 * rows)
        grad[i, two] = (dot(normed_t[i, two], err_t[...], 1, 1) * scale).astype(BF16)

    def add_into(i, where, *others):
        total = grad[i, where].astype(F32)
        for other in others:
            total = total + other[...].astype(F32)
        grad[i, where] = total.astype(BF16)

    def near(part, i):
        if i == 5:
            return (0, 0) if part == 0 else (FIRST, NEAR)
        return (0, FIRST) if part == 0 else (FIRST, rows - FIRST)

    def beyond(part):
        return (0, FIRST) if part == 0 else (FIRST + NEAR, rows - FIRST - NEAR)

    def at(dq, span):
        return pl.ds(SLOT[dq] * rows + span[0], span[1])

    def bottom(span):
        return span[0], span[1] // 2

    def top(span):
        return span[0] + span[1] // 2, span[1] // 2

    def slot_half(part, i):
        return pl.ds(0 if part == 0 else FIRST // 2, near(part, i)[1] // 2)

    def slot_far(part):
        return pl.ds(0 if part == 0 else FIRST, beyond(part)[1])

    sf, sx, p_half, p_whole, halves, wholes = {}, {}, {}, {}, {}, {}

    def take_far(i, part, *offsets):
        for dq in offsets if i == 4 else ():
            sf[part, dq].wait_recv()
            add_into(4, at(dq, beyond(part)), rx_far.at[dq, slot_far(part)])

    def give_far(i, part, *offsets):
        for dq in offsets if i == 5 else ():
            sf[part, dq] = send(
                grad.at[5, at(dq, beyond(part))], rx_far.at[dq, slot_far(part)],
                sf_s.at[part, dq], sf_r.at[part, dq], x_other,
            )

    def start_halves(i, part):
        take_far(i, part, 2)
        span = near(part, i)
        if span[1]:
            land = slot_half(part, i)
            s_sem, r_sem = sq_s.at[part, i], sq_r.at[part, i]
            halves[part, i] = (
                send(grad.at[i, at(2, bottom(span))], rq_half.at[i, 0, land], s_sem.at[0], r_sem.at[0], q_up),
                send(grad.at[i, at(2, top(span))], rq_half.at[i, 1, land], s_sem.at[1], r_sem.at[1], q_down),
            )

    def start_terms(i):
        terms(i, 2)
        give_far(i, 0, 2, 3)
        start_halves(i, 0)
        give_far(i, 1, 2)
        start_halves(i, 1)
        terms(i, 0)
        give_far(i, 0, 1, 0)
        give_far(i, 1, 3, 1, 0)

    def pass_on(i, part):
        take_far(i, part, 1, 3)
        span = near(part, i)
        if span[1]:
            land, rest = slot_half(part, i), pl.ds(*span)
            s_sem, r_sem = sq_s.at[part, i], sq_r.at[part, i]
            up, down = halves[part, i]
            up.wait_recv()
            add_into(i, at(1, bottom(span)), rq_half.at[i, 0, land])
            a = send(grad.at[i, at(1, span)], rq.at[i, 0, rest], s_sem.at[2], r_sem.at[2], q_up)
            down.wait_recv()
            add_into(i, at(3, top(span)), rq_half.at[i, 1, land])
            b = send(grad.at[i, at(3, span)], rq.at[i, 1, rest], s_sem.at[3], r_sem.at[3], q_down)
            wholes[part, i] = a, b

    def settle(i, part):
        span = near(part, i)
        if not span[1]:
            return
        for copy in wholes[part, i]:
            copy.wait_recv()
        dp, dx = i // 2, i % 2
        rest = pl.ds(*span)
        own = at(0, span)
        land = slot_half(part, i)
        up, down = p_up, p_down
        if dx:
            add_into(i, own, rq.at[i, 0, rest], rq.at[i, 1, rest])
            sx[part, dp] = send(
                grad.at[i, own], rx.at[dp, rest], sx_s.at[part, dp], sx_r.at[part, dp], x_other
            )
        elif dp == 2:
            take_far(4, part, 0)
            add_into(i, own, rq.at[i, 0, rest], rq.at[i, 1, rest])
            crossed = near(part, 5)
            if crossed[1]:
                sx[part, 2].wait_recv()
                add_into(i, at(0, crossed), rx.at[2, pl.ds(*crossed)])
            p_half[part, 0] = send(
                grad.at[i, at(0, bottom(span))], rp_half.at[0, land], sp_s.at[part, 0], sp_r.at[part, 0], up
            )
            p_half[part, 1] = send(
                grad.at[i, at(0, top(span))], rp_half.at[1, land], sp_s.at[part, 1], sp_r.at[part, 1], down
            )
        elif dp:
            sx[part, dp].wait_recv()
            add_into(i, own, rq.at[i, 0, rest], rq.at[i, 1, rest], rx.at[dp, rest])
            k = dp // 2
            p_half[part, k].wait_recv()
            add_into(i, at(0, (bottom, top)[k](span)), rp_half.at[k, land])
            p_whole[part, k] = send(
                grad.at[i, own], rp.at[k, rest], sp_s.at[part, 2 + k], sp_r.at[part, 2 + k], (up, down)[k]
            )

    def step_rows(part):
        span = near(part, 0)
        rest = pl.ds(*span)
        for copy in wholes[part, 0]:
            copy.wait_recv()
        sx[part, 0].wait_recv()
        total = grad[0, at(0, span)].astype(F32)
        for term in (rq.at[0, 0], rq.at[0, 1], rx.at[0]):
            total = total + term[rest].astype(F32)
        for k in (1, 0):
            p_whole[part, k].wait_recv()
            total = total + rp[k, rest].astype(F32)
        stepped_out[rest] = rolled[rest] - total

    pad = rows_out.shape[1]
    part_width = vocab // 4
    exchange, spread = [], []

    def my_columns(who):
        return pl.ds(pl.multiple_of(who * part_width, part_width), part_width)

    def start_sync():
        step_rows(0)
        for k in range(4):
            rows_out[k] = stepped_out[pl.ds(0, pad), k * part_width : (k + 1) * part_width]
        for j, to in enumerate(siblings):
            exchange.append(send(rows_out.at[to[0]], rows_in.at[j], e_s.at[j], e_r.at[j], to))

    def turn_sync():
        held = roll_up(anchor[...])[:pad]
        summed = rows_out[r]
        for j, copy in enumerate(exchange):
            copy.wait_recv()
            summed = summed + rows_in[j]
        delta = held - summed / 4
        moment = 0.9 * roll_up(momentum[...])[:pad] + delta
        moment_out[...] = moment
        fresh_rows = held - 0.7 * (delta + 0.9 * moment)
        new_out[...] = fresh_rows
        for j, to in enumerate(siblings):
            spread.append(send(new_out, new_in.at[j], n_s.at[j], n_r.at[j], to))
        fresh_out[:, my_columns(r)] = fresh_rows

    def end_sync():
        for j, copy in enumerate(spread):
            copy.wait_recv()
            fresh_out[:, my_columns(siblings[j][0])] = new_in[j]

    order = SCATTER_ORDER
    start_terms(order[0])
    for k, i in enumerate(order):
        if k + 1 < len(order):
            start_terms(order[k + 1])
        pass_on(i, 0)
        if k:
            settle(order[k - 1], 0)
    between = {2: start_sync, 4: turn_sync, 6: end_sync}
    for k, i in enumerate(order):
        pass_on(i, 1)
        if k:
            settle(order[k - 1], 1)
        if k in between:
            between[k]()
    step_rows(1)
    for copy in sent:
        copy.wait_send()


def merge(
    loss, stepped, fresh, moment, momentum, step_index, frag_table, loss_out, weights_out, momentum_out, rolled
):
    frag_count = frag_table.shape[0]
    rows = stepped.shape[0]
    run = rows // frag_count
    pad = fresh.shape[0]
    pos = step_index[0] % frag_count
    frag = jnp.int32(0)
    for k in range(frag_count):
        frag = frag + jnp.where(pos == k, frag_table[k], 0)
    offset = pl.multiple_of(frag * run // 8 * 8, 8)
    skip = frag * run - offset

    def synced(shape):
        row = lax.broadcasted_iota(jnp.int32, shape, 0)
        return (row >= skip) & (row < skip + run)

    loss_out[...] = loss[...]
    mixed = jnp.where(synced(fresh.shape), fresh[...], stepped[pl.ds(0, pad)])
    for k in range(2):
        rolled[pl.ds(k * rows, pad)] = mixed
        rolled[pl.ds(k * rows + pad, rows - pad)] = stepped[pl.ds(pad, rows - pad)]
    weights_out[...] = rolled[pl.ds(pl.multiple_of((rows - offset) % rows, 8), rows)]
    momentum_out[...] = momentum[...]
    momentum_out[pl.ds(offset, pad)] = jnp.where(synced(moment.shape), moment[...], momentum[pl.ds(offset, pad)])


def on_device(tokens, targets, norm_gain, weights, anchor, momentum, step_index, frag_table):
    _, count, width = tokens.shape
    _, rows, vocab = weights.shape
    half = rows // 2
    part = vocab // 4
    run = rows // frag_table.shape[0]
    pad = -(-run // 8) * 8
    vmem = pl.BlockSpec(memory_space=pltpu.VMEM)
    smem = pl.BlockSpec(memory_space=pltpu.SMEM)
    dma = pltpu.SemaphoreType.DMA
    big = pltpu.VMEM((8, 4 * rows, vocab), BF16)
    shapes = (
        jax.ShapeDtypeStruct((1, count), F32),
        jax.ShapeDtypeStruct((rows, vocab), F32),
        jax.ShapeDtypeStruct((rows, part), F32),
    )
    loss, stepped, fresh, moment = pl.pallas_call(
        kernel,
        out_shape=shapes[:2] + (jax.ShapeDtypeStruct((pad, vocab), F32), jax.ShapeDtypeStruct((pad, part), F32)),
        in_specs=[pl.BlockSpec(memory_space=pl.ANY)] + [vmem] * 5 + [smem] * 2,
        out_specs=(vmem,) * 4,
        scratch_shapes=[
            big,
            pltpu.VMEM((8, 4 * rows, count), BF16),
            big,
            pltpu.VMEM((vocab, count), F32),
            pltpu.VMEM((vocab, count), BF16),
            pltpu.VMEM((2, 128, width), BF16),
            pltpu.VMEM((8, 2, half, vocab), BF16),
            pltpu.VMEM((8, 2, rows, vocab), BF16),
            pltpu.VMEM((4, rows, vocab), BF16),
            pltpu.VMEM((4, rows - NEAR, vocab), BF16),
            pltpu.VMEM((2, half, vocab), BF16),
            pltpu.VMEM((2, rows, vocab), BF16),
            pltpu.VMEM((rows, vocab), F32),
            pltpu.VMEM((4, pad, part), F32),
            pltpu.VMEM((3, pad, part), F32),
            pltpu.VMEM((pad, part), F32),
            pltpu.VMEM((3, pad, part), F32),
            dma((2,)),
            dma((4,)), dma((4,)), dma((4,)), dma((4,)), dma((4,)), dma((4,)), dma((8, 4)), dma((8, 4)),
            dma((2, 4)), dma((2, 4)), dma((2, 4)), dma((2, 4)), dma((2, 4)), dma((2, 4)), dma((2, 8, 4)), dma((2, 8, 4)),
            dma((3,)), dma((3,)), dma((3,)), dma((3,)),
        ],
        compiler_params=pltpu.CompilerParams(
            collective_id=0, has_side_effects=True, vmem_limit_bytes=62 * 1024 * 1024
        ),
    )(
        tokens, targets, norm_gain[None], weights[0], anchor, momentum, step_index, frag_table
    )
    loss, weights_out, momentum_out = pl.pallas_call(
        merge, out_shape=shapes, in_specs=[vmem] * 5 + [smem] * 2, out_specs=(vmem,) * 3,
        scratch_shapes=[pltpu.VMEM((2 * rows, vocab), F32)],
    )(loss, stepped, fresh, moment, momentum, step_index, frag_table)
    return (loss, weights_out[None], momentum_out)


def solution(mesh):
    return jax.shard_map(
        on_device,
        mesh=mesh,
        in_specs=(
            P("rep", "fsdp", None),
            P("rep", "fsdp"),
            P(),
            P("rep", "fsdp", None),
            P("fsdp", "rep"),
            P("fsdp", "rep"),
            P(),
            P(),
        ),
        out_specs=(P("rep", "fsdp"), P("rep", "fsdp", None), P("fsdp", "rep")),
        check_vma=False,
    )
```

```python
import functools

import jax
import jax.numpy as jnp
import numpy as np
from jax import lax
from jax.experimental import pallas as pl
from jax.experimental.pallas import tpu as pltpu
from jax.sharding import PartitionSpec as P

F32 = jnp.float32
BF16 = jnp.bfloat16
MESH = pl.DeviceIdType.MESH

PLAN = (
    "T7", "h7", "T3", "P7", "h3", "T5", "h5", "p7",
    "T1", "p5", "h1", "T2", "h2", "T4", "p3", "T6",
    "P1", "T0", "P3", "S7", "P4", "h6", "P6", "S1",
    "h0", "P0", "S4", "s5", "P2", "p1", "h4", "S6",
    "S3", "s3", "p6", "S2", "s7", "p4", "X0", "p2",
    "s4", "s1", "p0", "X1", "s2", "s6", "X2",
)
FIRST = 32
ROLL = (16, 40, 80)
SLOT = (0, 1, 3, 2)
NEAR = 64


def dot(a, b, ca, cb):
    return lax.dot_general(a, b, (((ca,), (cb,)), ((), ())), preferred_element_type=F32)


def kernel(
    tokens, targets, gain, weights, anchor, momentum, step_index, frag_table,
    loss_out, stepped_out, fresh_out, moment_out,
    head, normed_t, grad, logits_t, err_t, tok, rq_half, rq, rx, rx_far, rp_half, rp, rolled, rows_out, rows_in, new_out, new_in,
    tok_sem, gp_s, gp_r, gx_s, gx_r, gf_s, gf_r, gq_s, gq_r,
    sp_s, sp_r, sx_s, sx_r, sf_s, sf_r, sq_s, sq_r, e_s, e_r, n_s, n_r,
):
    rows, vocab = weights.shape
    half = rows // 2
    count, width = tokens.shape[1:]
    frag_count = frag_table.shape[0]
    run = rows // frag_count
    chunk = tok.shape[1]
    scale = np.float32(1.0 / np.sqrt(np.float32(width)))

    r, f = lax.axis_index("rep"), lax.axis_index("fsdp")
    core = r % 2
    z, y, x = f // 8, (f // 2) % 4, f % 2
    p = jnp.where(core == 0, z, y)
    q = jnp.where(core == 0, y, z)

    def device(dp=0, dq=0, dx=0):
        pp, qq, xx = (p + dp) % 4, (q + dq) % 4, (x + dx) % 2
        return (r, jnp.where(core == 0, pp, qq) * 8 + jnp.where(core == 0, qq, pp) * 2 + xx)

    p_up, p_down, q_up, q_down, x_other = device(dp=1), device(dp=3), device(dq=1), device(dq=3), device(dx=1)

    def sibling(j):
        c2, l2 = (core + j) % 2, (r // 2 + j // 2) % 2
        return l2 * 2 + c2

    siblings = [(sibling(j), f) for j in (1, 2, 3)]

    barrier = pltpu.get_barrier_semaphore()
    partners = [p_up, p_down, q_up, q_down, x_other] + siblings
    for partner in partners:
        pl.semaphore_signal(barrier, inc=1, device_id=partner, device_id_type=MESH)

    chunks = count // chunk
    slots = tok.shape[0]

    def token_copy(c):
        return pltpu.make_async_copy(
            tokens.at[0, pl.ds(c * chunk, chunk)], tok.at[c % slots], tok_sem.at[c % slots]
        )

    for c in range(slots):
        token_copy(c).start()
    pos = step_index[0] % frag_count
    frag = jnp.int32(0)
    for k in range(frag_count):
        frag = frag + jnp.where(pos == k, frag_table[k], 0)
    bits = [frag % 2 == 1, frag // 2 % 2 == 1, frag // 4 == 1]

    def roll_up(value):
        for bit, step in zip(bits, ROLL):
            value = jnp.where(bit, jnp.concatenate([value[step:], value[:step]]), value)
        return value

    rolled[...] = roll_up(weights[...])
    head[0, pl.ds(0, rows)] = rolled[...].astype(BF16)
    pl.semaphore_wait(barrier, len(partners))

    sent = []

    def send(src, dst, s_sem, r_sem, to):
        copy = pltpu.make_async_remote_copy(
            src_ref=src, dst_ref=dst, send_sem=s_sem, recv_sem=r_sem, device_id=to, device_id_type=MESH
        )
        copy.start()
        sent.append(copy)
        return copy

    def whole(dq, i=0):
        return pl.ds(SLOT[dq] * rows, NEAR if i == 5 else rows)

    def low(dq, i=0):
        return pl.ds(SLOT[dq] * rows, NEAR // 2 if i == 5 else half)

    def high(dq, i=0):
        cut = NEAR // 2 if i == 5 else half
        return pl.ds(SLOT[dq] * rows + cut, cut)

    def far(dq):
        return pl.ds(SLOT[dq] * rows + NEAR, rows - NEAR)

    def gather_q(i):
        a = send(head.at[i, whole(0, i)], head.at[i, whole(3, i)], gq_s.at[i, 0], gq_r.at[i, 0], q_up)
        b = send(head.at[i, whole(0, i)], head.at[i, whole(1, i)], gq_s.at[i, 1], gq_r.at[i, 1], q_down)
        return a, b

    def forward_q(i, pair):
        pair[0].wait_recv()
        a = send(head.at[i, low(3, i)], head.at[i, low(2, i)], gq_s.at[i, 2], gq_r.at[i, 2], q_up)
        pair[1].wait_recv()
        b = send(head.at[i, high(1, i)], head.at[i, high(2, i)], gq_s.at[i, 3], gq_r.at[i, 3], q_down)
        return a, b

    def gather_x(dp):
        i = 2 * dp
        return send(head.at[i, whole(0, i + 1)], head.at[i + 1, whole(0, i + 1)], gx_s.at[dp], gx_r.at[dp], x_other)

    def gather_far(dq):
        return send(head.at[4, far(dq)], head.at[5, far(dq)], gf_s.at[dq], gf_r.at[dq], x_other)

    def norm_chunk(c, slot):
        xf = tok[slot].astype(F32)
        inv = lax.rsqrt(jnp.sum(xf * xf, axis=1, keepdims=True) * np.float32(1.0 / width) + np.float32(1e-5))

        def unit(j, carry):
            columns = pl.ds(pl.multiple_of(j * 4 * rows, 128), 4 * rows)
            part = (tok[slot, :, columns].astype(F32) * inv * gain[:, columns]).T
            for b in range(4):
                bz, by, bx = j // 2, 2 * (j % 2) + b // 2, b % 2
                dp = (jnp.where(core == 0, bz, by) - p + 4) % 4
                dq = (jnp.where(core == 0, by, bz) - q + 4) % 4
                dx = (bx + x) % 2
                normed_t[
                    2 * dp + dx,
                    pl.ds(pl.multiple_of((dq ^ (dq >> 1)) * rows, 16), rows),
                    pl.ds(pl.multiple_of(c * chunk, chunk), chunk),
                ] = roll_up(part[b * rows : (b + 1) * rows]).astype(BF16)
            return carry

        lax.fori_loop(0, width // (4 * rows), unit, 0)

    def norm(first, last):
        for c in range(first, last):
            token_copy(c).wait()
            norm_chunk(c, c % slots)
            if c + slots < chunks:
                token_copy(c + slots).start()

    early = pl.ds(0, 3 * rows)
    last = pl.ds(3 * rows, rows)

    def add_logits(i, where=pl.ds(0, 4 * rows), fresh=False):
        tile = vocab // 2

        def step(j, carry):
            s = pl.ds(pl.multiple_of(j * tile, tile), tile)
            term = dot(head[i, where, s], normed_t[i, where], 0, 0)
            if fresh:
                logits_t[s, :] = term
            else:
                logits_t[s, :] += term
            return carry

        lax.fori_loop(0, vocab // tile, step, 0)

    def settle_q(i):
        fq[i][0].wait_recv()
        fq[i][1].wait_recv()

    def finish(i, fresh=False):
        settle_q(i)
        add_logits(i, fresh=fresh)

    own = head.at[0, whole(0)]
    up = send(own, head.at[6, whole(0)], gp_s.at[0], gp_r.at[0], p_up)
    down = send(own, head.at[2, whole(0)], gp_s.at[1], gp_r.at[1], p_down)
    gx, gq, fq, gf = {0: gather_x(0)}, {0: gather_q(0)}, {}, {}
    norm(0, 4)
    up.wait_recv()
    up2 = send(head.at[6, low(0)], head.at[4, low(0)], gp_s.at[2], gp_r.at[2], p_up)
    down.wait_recv()
    down2 = send(head.at[2, high(0)], head.at[4, high(0)], gp_s.at[3], gp_r.at[3], p_down)
    gx[1] = gather_x(1)
    gx[3] = gather_x(3)
    gq[2] = gather_q(2)
    gq[6] = gather_q(6)
    norm(4, 6)
    fq[0] = forward_q(0, gq[0])
    up2.wait_recv()
    down2.wait_recv()
    gq[4] = gather_q(4)
    gx[2] = gather_x(2)
    gf[0] = gather_far(0)
    gx[0].wait_recv()
    gq[1] = gather_q(1)
    norm(6, 8)
    fq[2] = forward_q(2, gq[2])
    fq[6] = forward_q(6, gq[6])
    finish(0, fresh=True)
    fq[4] = forward_q(4, gq[4])
    gf[1] = gather_far(1)
    gf[3] = gather_far(3)
    gx[1].wait_recv()
    gq[3] = gather_q(3)
    finish(2)
    fq[4][0].wait_recv()
    fq[4][1].wait_recv()
    gf[2] = gather_far(2)
    gx[3].wait_recv()
    gq[7] = gather_q(7)
    fq[1] = forward_q(1, gq[1])
    finish(6)
    gx[2].wait_recv()
    gq[5] = gather_q(5)
    fq[3] = forward_q(3, gq[3])
    add_logits(4)
    fq[7] = forward_q(7, gq[7])
    finish(1)
    fq[5] = forward_q(5, gq[5])
    add_logits(3, early)
    add_logits(7, early)
    for dq in (0, 1, 3):
        gf[dq].wait_recv()
    add_logits(5, early)
    gf[2].wait_recv()
    tail = (3, 7, 5)
    for i in tail:
        settle_q(i)
    logits_t[...] += dot(
        jnp.concatenate([head[i, last] for i in tail]), jnp.concatenate([normed_t[i, last] for i in tail]), 0, 0
    )

    lanes = 128

    def soften(j, carry):
        s = pl.ds(pl.multiple_of(j * lanes, lanes), lanes)
        logit = logits_t[:, s] * scale
        expo = jnp.exp(logit)
        total = jnp.sum(expo, axis=0, keepdims=True)
        onehot = lax.broadcasted_iota(jnp.int32, (vocab, lanes), 0) == targets[:, s]
        picked = jnp.sum(jnp.where(onehot, logit, 0.0), axis=0, keepdims=True)
        loss_out[:, s] = jnp.log(total) - picked
        err_t[:, s] = (expo * (1.0 / total) - jnp.where(onehot, 1.0, 0.0)).astype(BF16)
        return carry

    lax.fori_loop(0, count // lanes, soften, 0)

    def terms(i, slot):
        two = pl.ds(slot * rows, 2 * rows)
        grad[i, two] = (dot(normed_t[i, two], err_t[...], 1, 1) * scale).astype(BF16)

    def add_into(i, where, *others):
        total = grad[i, where].astype(F32)
        for other in others:
            total = total + other[...].astype(F32)
        grad[i, where] = total.astype(BF16)

    def near(part, i):
        if i == 5:
            return (0, 0) if part == 0 else (FIRST, NEAR)
        return (0, FIRST) if part == 0 else (FIRST, rows - FIRST)

    def beyond(part):
        return (0, FIRST) if part == 0 else (FIRST + NEAR, rows - FIRST - NEAR)

    def at(dq, span):
        return pl.ds(SLOT[dq] * rows + span[0], span[1])

    def bottom(span):
        return span[0], span[1] // 2

    def top(span):
        return span[0] + span[1] // 2, span[1] // 2

    def slot_half(part, i):
        return pl.ds(0 if part == 0 else FIRST // 2, near(part, i)[1] // 2)

    def slot_far(part):
        return pl.ds(0 if part == 0 else FIRST, beyond(part)[1])

    sf, sx, p_half, p_whole, halves, wholes = {}, {}, {}, {}, {}, {}

    def take_far(i, part, *offsets):
        for dq in offsets if i == 4 else ():
            sf[part, dq].wait_recv()
            add_into(4, at(dq, beyond(part)), rx_far.at[dq, slot_far(part)])

    def give_far(i, part, *offsets):
        for dq in offsets if i == 5 else ():
            sf[part, dq] = send(
                grad.at[5, at(dq, beyond(part))], rx_far.at[dq, slot_far(part)],
                sf_s.at[part, dq], sf_r.at[part, dq], x_other,
            )

    def start_halves(i, part):
        take_far(i, part, 2)
        span = near(part, i)
        if span[1]:
            land = slot_half(part, i)
            s_sem, r_sem = sq_s.at[part, i], sq_r.at[part, i]
            halves[part, i] = (
                send(grad.at[i, at(2, bottom(span))], rq_half.at[i, 0, land], s_sem.at[0], r_sem.at[0], q_up),
                send(grad.at[i, at(2, top(span))], rq_half.at[i, 1, land], s_sem.at[1], r_sem.at[1], q_down),
            )

    def start_terms(i):
        terms(i, 2)
        give_far(i, 0, 2, 3)
        start_halves(i, 0)
        terms(i, 0)
        give_far(i, 0, 1, 0)

    def start_rest(i):
        give_far(i, 1, 2)
        start_halves(i, 1)
        give_far(i, 1, 3, 1, 0)

    def pass_on(i, part):
        take_far(i, part, 1, 3)
        span = near(part, i)
        if span[1]:
            land, rest = slot_half(part, i), pl.ds(*span)
            s_sem, r_sem = sq_s.at[part, i], sq_r.at[part, i]
            up, down = halves[part, i]
            up.wait_recv()
            add_into(i, at(1, bottom(span)), rq_half.at[i, 0, land])
            a = send(grad.at[i, at(1, span)], rq.at[i, 0, rest], s_sem.at[2], r_sem.at[2], q_up)
            down.wait_recv()
            add_into(i, at(3, top(span)), rq_half.at[i, 1, land])
            b = send(grad.at[i, at(3, span)], rq.at[i, 1, rest], s_sem.at[3], r_sem.at[3], q_down)
            wholes[part, i] = a, b

    def settle(i, part):
        span = near(part, i)
        if not span[1]:
            return
        for copy in wholes[part, i]:
            copy.wait_recv()
        dp, dx = i // 2, i % 2
        rest = pl.ds(*span)
        own = at(0, span)
        land = slot_half(part, i)
        up, down = p_up, p_down
        if dx:
            add_into(i, own, rq.at[i, 0, rest], rq.at[i, 1, rest])
            sx[part, dp] = send(
                grad.at[i, own], rx.at[dp, rest], sx_s.at[part, dp], sx_r.at[part, dp], x_other
            )
        elif dp == 2:
            take_far(4, part, 0)
            add_into(i, own, rq.at[i, 0, rest], rq.at[i, 1, rest])
            crossed = near(part, 5)
            if crossed[1]:
                sx[part, 2].wait_recv()
                add_into(i, at(0, crossed), rx.at[2, pl.ds(*crossed)])
            p_half[part, 0] = send(
                grad.at[i, at(0, bottom(span))], rp_half.at[0, land], sp_s.at[part, 0], sp_r.at[part, 0], up
            )
            p_half[part, 1] = send(
                grad.at[i, at(0, top(span))], rp_half.at[1, land], sp_s.at[part, 1], sp_r.at[part, 1], down
            )
        elif dp:
            sx[part, dp].wait_recv()
            add_into(i, own, rq.at[i, 0, rest], rq.at[i, 1, rest], rx.at[dp, rest])
            k = dp // 2
            p_half[part, k].wait_recv()
            add_into(i, at(0, (bottom, top)[k](span)), rp_half.at[k, land])
            p_whole[part, k] = send(
                grad.at[i, own], rp.at[k, rest], sp_s.at[part, 2 + k], sp_r.at[part, 2 + k], (up, down)[k]
            )

    def step_rows(part):
        span = near(part, 0)
        rest = pl.ds(*span)
        for copy in wholes[part, 0]:
            copy.wait_recv()
        sx[part, 0].wait_recv()
        total = grad[0, at(0, span)].astype(F32)
        for term in (rq.at[0, 0], rq.at[0, 1], rx.at[0]):
            total = total + term[rest].astype(F32)
        for k in (1, 0):
            p_whole[part, k].wait_recv()
            total = total + rp[k, rest].astype(F32)
        stepped_out[rest] = rolled[rest] - total

    pad = rows_out.shape[1]
    part_width = vocab // 4
    exchange, spread = [], []

    def my_columns(who):
        return pl.ds(pl.multiple_of(who * part_width, part_width), part_width)

    def start_sync():
        step_rows(0)
        for k in range(4):
            rows_out[k] = stepped_out[pl.ds(0, pad), k * part_width : (k + 1) * part_width]
        for j, to in enumerate(siblings):
            exchange.append(send(rows_out.at[to[0]], rows_in.at[j], e_s.at[j], e_r.at[j], to))

    def turn_sync():
        held = roll_up(anchor[...])[:pad]
        summed = rows_out[r]
        for j, copy in enumerate(exchange):
            copy.wait_recv()
            summed = summed + rows_in[j]
        delta = held - summed / 4
        moment = 0.9 * roll_up(momentum[...])[:pad] + delta
        moment_out[...] = moment
        fresh_rows = held - 0.7 * (delta + 0.9 * moment)
        new_out[...] = fresh_rows
        for j, to in enumerate(siblings):
            spread.append(send(new_out, new_in.at[j], n_s.at[j], n_r.at[j], to))
        fresh_out[:, my_columns(r)] = fresh_rows

    def end_sync():
        for j, copy in enumerate(spread):
            copy.wait_recv()
            fresh_out[:, my_columns(siblings[j][0])] = new_in[j]

    act = {
        "T": start_terms,
        "h": start_rest,
        "P": lambda i: pass_on(i, 0),
        "S": lambda i: settle(i, 0),
        "p": lambda i: pass_on(i, 1),
        "s": lambda i: settle(i, 1),
        "X": lambda i: (start_sync, turn_sync, end_sync)[i](),
    }
    for step in PLAN:
        act[step[0]](int(step[1]))
    step_rows(1)
    for copy in sent:
        copy.wait_send()


def merge(
    loss, stepped, fresh, moment, momentum, step_index, frag_table, loss_out, weights_out, momentum_out, rolled
):
    frag_count = frag_table.shape[0]
    rows = stepped.shape[0]
    run = rows // frag_count
    pad = fresh.shape[0]
    pos = step_index[0] % frag_count
    frag = jnp.int32(0)
    for k in range(frag_count):
        frag = frag + jnp.where(pos == k, frag_table[k], 0)
    offset = pl.multiple_of(frag * run // 8 * 8, 8)
    skip = frag * run - offset

    def synced(shape):
        row = lax.broadcasted_iota(jnp.int32, shape, 0)
        return (row >= skip) & (row < skip + run)

    loss_out[...] = loss[...]
    mixed = jnp.where(synced(fresh.shape), fresh[...], stepped[pl.ds(0, pad)])
    for k in range(2):
        rolled[pl.ds(k * rows, pad)] = mixed
        rolled[pl.ds(k * rows + pad, rows - pad)] = stepped[pl.ds(pad, rows - pad)]
    weights_out[...] = rolled[pl.ds(pl.multiple_of((rows - offset) % rows, 8), rows)]
    momentum_out[...] = momentum[...]
    momentum_out[pl.ds(offset, pad)] = jnp.where(synced(moment.shape), moment[...], momentum[pl.ds(offset, pad)])


def on_device(tokens, targets, norm_gain, weights, anchor, momentum, step_index, frag_table):
    _, count, width = tokens.shape
    _, rows, vocab = weights.shape
    half = rows // 2
    part = vocab // 4
    run = rows // frag_table.shape[0]
    pad = -(-run // 8) * 8
    vmem = pl.BlockSpec(memory_space=pltpu.VMEM)
    smem = pl.BlockSpec(memory_space=pltpu.SMEM)
    dma = pltpu.SemaphoreType.DMA
    big = pltpu.VMEM((8, 4 * rows, vocab), BF16)
    shapes = (
        jax.ShapeDtypeStruct((1, count), F32),
        jax.ShapeDtypeStruct((rows, vocab), F32),
        jax.ShapeDtypeStruct((rows, part), F32),
    )
    loss, stepped, fresh, moment = pl.pallas_call(
        kernel,
        out_shape=shapes[:2] + (jax.ShapeDtypeStruct((pad, vocab), F32), jax.ShapeDtypeStruct((pad, part), F32)),
        in_specs=[pl.BlockSpec(memory_space=pl.ANY)] + [vmem] * 5 + [smem] * 2,
        out_specs=(vmem,) * 4,
        scratch_shapes=[
            big,
            pltpu.VMEM((8, 4 * rows, count), BF16),
            big,
            pltpu.VMEM((vocab, count), F32),
            pltpu.VMEM((vocab, count), BF16),
            pltpu.VMEM((2, 128, width), BF16),
            pltpu.VMEM((8, 2, half, vocab), BF16),
            pltpu.VMEM((8, 2, rows, vocab), BF16),
            pltpu.VMEM((4, rows, vocab), BF16),
            pltpu.VMEM((4, rows - NEAR, vocab), BF16),
            pltpu.VMEM((2, half, vocab), BF16),
            pltpu.VMEM((2, rows, vocab), BF16),
            pltpu.VMEM((rows, vocab), F32),
            pltpu.VMEM((4, pad, part), F32),
            pltpu.VMEM((3, pad, part), F32),
            pltpu.VMEM((pad, part), F32),
            pltpu.VMEM((3, pad, part), F32),
            dma((2,)),
            dma((4,)), dma((4,)), dma((4,)), dma((4,)), dma((4,)), dma((4,)), dma((8, 4)), dma((8, 4)),
            dma((2, 4)), dma((2, 4)), dma((2, 4)), dma((2, 4)), dma((2, 4)), dma((2, 4)), dma((2, 8, 4)), dma((2, 8, 4)),
            dma((3,)), dma((3,)), dma((3,)), dma((3,)),
        ],
        compiler_params=pltpu.CompilerParams(
            collective_id=0, has_side_effects=True, vmem_limit_bytes=62 * 1024 * 1024
        ),
    )(
        tokens, targets, norm_gain[None], weights[0], anchor, momentum, step_index, frag_table
    )
    loss, weights_out, momentum_out = pl.pallas_call(
        merge, out_shape=shapes, in_specs=[vmem] * 5 + [smem] * 2, out_specs=(vmem,) * 3,
        scratch_shapes=[pltpu.VMEM((2 * rows, vocab), F32)],
    )(loss, stepped, fresh, moment, momentum, step_index, frag_table)
    return (loss, weights_out[None], momentum_out)


def solution(mesh):
    return jax.shard_map(
        on_device,
        mesh=mesh,
        in_specs=(
            P("rep", "fsdp", None),
            P("rep", "fsdp"),
            P(),
            P("rep", "fsdp", None),
            P("fsdp", "rep"),
            P("fsdp", "rep"),
            P(),
            P(),
        ),
        out_specs=(P("rep", "fsdp"), P("rep", "fsdp", None), P("fsdp", "rep")),
        check_vma=False,
    )
```

```python
import functools

import jax
import jax.numpy as jnp
import numpy as np
from jax import lax
from jax.experimental import pallas as pl
from jax.experimental.pallas import tpu as pltpu
from jax.sharding import PartitionSpec as P

F32 = jnp.float32
BF16 = jnp.bfloat16
MESH = pl.DeviceIdType.MESH

PLAN = (
    "T7", "h7", "T3", "P7", "h3", "T5", "h5", "p7",
    "T1", "p5", "h1", "T2", "h2", "T4", "p3", "T6",
    "P1", "T0", "P3", "S7", "P4", "h6", "P6", "S1",
    "h0", "P0", "S4", "s5", "P2", "p1", "h4", "S6",
    "S3", "s3", "p6", "S2", "s7", "p4", "X0", "p2",
    "s4", "s1", "p0", "X1", "s2", "s6", "X2",
)
FIRST = 32
ROLL = (16, 40, 80)
SLOT = (0, 1, 3, 2)
NEAR = 64


def dot(a, b, ca, cb):
    return lax.dot_general(a, b, (((ca,), (cb,)), ((), ())), preferred_element_type=F32)


def kernel(
    tokens, targets_in, gain_in, weights_in, anchor_in, momentum_in, step_in, table_in,
    loss_out, stepped_out, fresh_out, moment_out,
    head, normed_t, grad, logits_t, err_t, tok, rq_half, rq, rx, rx_far, rp_half, rp, rolled, rows_out, rows_in, new_out, new_in,
    targets, gain, weights, anchor, momentum, step_index, frag_table, load_sem, tok_sem, gp_s, gp_r, gx_s, gx_r, gf_s, gf_r, gq_s, gq_r,
    sp_s, sp_r, sx_s, sx_r, sf_s, sf_r, sq_s, sq_r, e_s, e_r, n_s, n_r,
):
    rows, vocab = weights.shape
    half = rows // 2
    count, width = tokens.shape[1:]
    frag_count = frag_table.shape[0]
    run = rows // frag_count
    chunk = tok.shape[1]
    scale = np.float32(1.0 / np.sqrt(np.float32(width)))

    r, f = lax.axis_index("rep"), lax.axis_index("fsdp")
    core = r % 2
    z, y, x = f // 8, (f // 2) % 4, f % 2
    p = jnp.where(core == 0, z, y)
    q = jnp.where(core == 0, y, z)

    def device(dp=0, dq=0, dx=0):
        pp, qq, xx = (p + dp) % 4, (q + dq) % 4, (x + dx) % 2
        return (r, jnp.where(core == 0, pp, qq) * 8 + jnp.where(core == 0, qq, pp) * 2 + xx)

    p_up, p_down, q_up, q_down, x_other = device(dp=1), device(dp=3), device(dq=1), device(dq=3), device(dx=1)

    def sibling(j):
        c2, l2 = (core + j) % 2, (r // 2 + j // 2) % 2
        return l2 * 2 + c2

    siblings = [(sibling(j), f) for j in (1, 2, 3)]

    barrier = pltpu.get_barrier_semaphore()
    partners = [p_up, p_down, q_up, q_down, x_other] + siblings
    for partner in partners:
        pl.semaphore_signal(barrier, inc=1, device_id=partner, device_id_type=MESH)

    chunks = count // chunk
    slots = tok.shape[0]

    def token_copy(c):
        return pltpu.make_async_copy(
            tokens.at[0, pl.ds(c * chunk, chunk)], tok.at[c % slots], tok_sem.at[c % slots]
        )

    pairs = (
        (step_in, step_index), (table_in, frag_table), (weights_in, weights), (gain_in, gain),
        (targets_in, targets), (anchor_in, anchor), (momentum_in, momentum),
    )
    loads = [pltpu.make_async_copy(src, dst, load_sem.at[k]) for k, (src, dst) in enumerate(pairs)]
    for load in loads[:3]:
        load.start()
    for c in range(slots):
        token_copy(c).start()
    for load in loads[3:]:
        load.start()
    for load in loads[:3]:
        load.wait()
    pos = step_index[0] % frag_count
    frag = jnp.int32(0)
    for k in range(frag_count):
        frag = frag + jnp.where(pos == k, frag_table[k], 0)
    bits = [frag % 2 == 1, frag // 2 % 2 == 1, frag // 4 == 1]

    def roll_up(value):
        for bit, step in zip(bits, ROLL):
            value = jnp.where(bit, jnp.concatenate([value[step:], value[:step]]), value)
        return value

    rolled[...] = roll_up(weights[...])
    head[0, pl.ds(0, rows)] = rolled[...].astype(BF16)
    pl.semaphore_wait(barrier, len(partners))

    sent = []

    def send(src, dst, s_sem, r_sem, to):
        copy = pltpu.make_async_remote_copy(
            src_ref=src, dst_ref=dst, send_sem=s_sem, recv_sem=r_sem, device_id=to, device_id_type=MESH
        )
        copy.start()
        sent.append(copy)
        return copy

    def whole(dq, i=0):
        return pl.ds(SLOT[dq] * rows, NEAR if i == 5 else rows)

    def low(dq, i=0):
        return pl.ds(SLOT[dq] * rows, NEAR // 2 if i == 5 else half)

    def high(dq, i=0):
        cut = NEAR // 2 if i == 5 else half
        return pl.ds(SLOT[dq] * rows + cut, cut)

    def far(dq):
        return pl.ds(SLOT[dq] * rows + NEAR, rows - NEAR)

    def gather_q(i):
        a = send(head.at[i, whole(0, i)], head.at[i, whole(3, i)], gq_s.at[i, 0], gq_r.at[i, 0], q_up)
        b = send(head.at[i, whole(0, i)], head.at[i, whole(1, i)], gq_s.at[i, 1], gq_r.at[i, 1], q_down)
        return a, b

    def forward_q(i, pair):
        pair[0].wait_recv()
        a = send(head.at[i, low(3, i)], head.at[i, low(2, i)], gq_s.at[i, 2], gq_r.at[i, 2], q_up)
        pair[1].wait_recv()
        b = send(head.at[i, high(1, i)], head.at[i, high(2, i)], gq_s.at[i, 3], gq_r.at[i, 3], q_down)
        return a, b

    def gather_x(dp):
        i = 2 * dp
        return send(head.at[i, whole(0, i + 1)], head.at[i + 1, whole(0, i + 1)], gx_s.at[dp], gx_r.at[dp], x_other)

    def gather_far(dq):
        return send(head.at[4, far(dq)], head.at[5, far(dq)], gf_s.at[dq], gf_r.at[dq], x_other)

    def norm_chunk(c, slot):
        xf = tok[slot].astype(F32)
        inv = lax.rsqrt(jnp.sum(xf * xf, axis=1, keepdims=True) * np.float32(1.0 / width) + np.float32(1e-5))

        def unit(j, carry):
            columns = pl.ds(pl.multiple_of(j * 4 * rows, 128), 4 * rows)
            part = (tok[slot, :, columns].astype(F32) * inv * gain[:, columns]).T
            for b in range(4):
                bz, by, bx = j // 2, 2 * (j % 2) + b // 2, b % 2
                dp = (jnp.where(core == 0, bz, by) - p + 4) % 4
                dq = (jnp.where(core == 0, by, bz) - q + 4) % 4
                dx = (bx + x) % 2
                normed_t[
                    2 * dp + dx,
                    pl.ds(pl.multiple_of((dq ^ (dq >> 1)) * rows, 16), rows),
                    pl.ds(pl.multiple_of(c * chunk, chunk), chunk),
                ] = roll_up(part[b * rows : (b + 1) * rows]).astype(BF16)
            return carry

        lax.fori_loop(0, width // (4 * rows), unit, 0)

    def norm(first, last):
        for c in range(first, last):
            token_copy(c).wait()
            norm_chunk(c, c % slots)
            if c + slots < chunks:
                token_copy(c + slots).start()

    early = pl.ds(0, 3 * rows)
    last = pl.ds(3 * rows, rows)

    def add_logits(i, where=pl.ds(0, 4 * rows), fresh=False):
        tile = vocab // 2

        def step(j, carry):
            s = pl.ds(pl.multiple_of(j * tile, tile), tile)
            term = dot(head[i, where, s], normed_t[i, where], 0, 0)
            if fresh:
                logits_t[s, :] = term
            else:
                logits_t[s, :] += term
            return carry

        lax.fori_loop(0, vocab // tile, step, 0)

    def settle_q(i):
        fq[i][0].wait_recv()
        fq[i][1].wait_recv()

    def finish(i, fresh=False):
        settle_q(i)
        add_logits(i, fresh=fresh)

    own = head.at[0, whole(0)]
    up = send(own, head.at[6, whole(0)], gp_s.at[0], gp_r.at[0], p_up)
    down = send(own, head.at[2, whole(0)], gp_s.at[1], gp_r.at[1], p_down)
    gx, gq, fq, gf = {0: gather_x(0)}, {0: gather_q(0)}, {}, {}
    for load in loads[3:]:
        load.wait()
    norm(0, 4)
    up.wait_recv()
    up2 = send(head.at[6, low(0)], head.at[4, low(0)], gp_s.at[2], gp_r.at[2], p_up)
    down.wait_recv()
    down2 = send(head.at[2, high(0)], head.at[4, high(0)], gp_s.at[3], gp_r.at[3], p_down)
    gx[1] = gather_x(1)
    gx[3] = gather_x(3)
    gq[2] = gather_q(2)
    gq[6] = gather_q(6)
    norm(4, 6)
    fq[0] = forward_q(0, gq[0])
    up2.wait_recv()
    down2.wait_recv()
    gq[4] = gather_q(4)
    gx[2] = gather_x(2)
    gf[0] = gather_far(0)
    gx[0].wait_recv()
    gq[1] = gather_q(1)
    norm(6, 8)
    fq[2] = forward_q(2, gq[2])
    fq[6] = forward_q(6, gq[6])
    finish(0, fresh=True)
    fq[4] = forward_q(4, gq[4])
    gf[1] = gather_far(1)
    gf[3] = gather_far(3)
    gx[1].wait_recv()
    gq[3] = gather_q(3)
    finish(2)
    fq[4][0].wait_recv()
    fq[4][1].wait_recv()
    gf[2] = gather_far(2)
    gx[3].wait_recv()
    gq[7] = gather_q(7)
    fq[1] = forward_q(1, gq[1])
    finish(6)
    gx[2].wait_recv()
    gq[5] = gather_q(5)
    fq[3] = forward_q(3, gq[3])
    add_logits(4)
    fq[7] = forward_q(7, gq[7])
    finish(1)
    fq[5] = forward_q(5, gq[5])
    add_logits(3, early)
    add_logits(7, early)
    for dq in (0, 1, 3):
        gf[dq].wait_recv()
    add_logits(5, early)
    gf[2].wait_recv()
    tail = (3, 7, 5)
    for i in tail:
        settle_q(i)
    logits_t[...] += dot(
        jnp.concatenate([head[i, last] for i in tail]), jnp.concatenate([normed_t[i, last] for i in tail]), 0, 0
    )

    lanes = 128

    def soften(j, carry):
        s = pl.ds(pl.multiple_of(j * lanes, lanes), lanes)
        logit = logits_t[:, s] * scale
        expo = jnp.exp(logit)
        total = jnp.sum(expo, axis=0, keepdims=True)
        onehot = lax.broadcasted_iota(jnp.int32, (vocab, lanes), 0) == targets[:, s]
        picked = jnp.sum(jnp.where(onehot, logit, 0.0), axis=0, keepdims=True)
        loss_out[:, s] = jnp.log(total) - picked
        err_t[:, s] = (expo * (1.0 / total) - jnp.where(onehot, 1.0, 0.0)).astype(BF16)
        return carry

    lax.fori_loop(0, count // lanes, soften, 0)

    def terms(i, slot):
        two = pl.ds(slot * rows, 2 * rows)
        grad[i, two] = (dot(normed_t[i, two], err_t[...], 1, 1) * scale).astype(BF16)

    def add_into(i, where, *others):
        total = grad[i, where].astype(F32)
        for other in others:
            total = total + other[...].astype(F32)
        grad[i, where] = total.astype(BF16)

    def near(part, i):
        if i == 5:
            return (0, 0) if part == 0 else (FIRST, NEAR)
        return (0, FIRST) if part == 0 else (FIRST, rows - FIRST)

    def beyond(part):
        return (0, FIRST) if part == 0 else (FIRST + NEAR, rows - FIRST - NEAR)

    def at(dq, span):
        return pl.ds(SLOT[dq] * rows + span[0], span[1])

    def bottom(span):
        return span[0], span[1] // 2

    def top(span):
        return span[0] + span[1] // 2, span[1] // 2

    def slot_half(part, i):
        return pl.ds(0 if part == 0 else FIRST // 2, near(part, i)[1] // 2)

    def slot_far(part):
        return pl.ds(0 if part == 0 else FIRST, beyond(part)[1])

    sf, sx, p_half, p_whole, halves, wholes = {}, {}, {}, {}, {}, {}

    def take_far(i, part, *offsets):
        for dq in offsets if i == 4 else ():
            sf[part, dq].wait_recv()
            add_into(4, at(dq, beyond(part)), rx_far.at[dq, slot_far(part)])

    def give_far(i, part, *offsets):
        for dq in offsets if i == 5 else ():
            sf[part, dq] = send(
                grad.at[5, at(dq, beyond(part))], rx_far.at[dq, slot_far(part)],
                sf_s.at[part, dq], sf_r.at[part, dq], x_other,
            )

    def start_halves(i, part):
        take_far(i, part, 2)
        span = near(part, i)
        if span[1]:
            land = slot_half(part, i)
            s_sem, r_sem = sq_s.at[part, i], sq_r.at[part, i]
            halves[part, i] = (
                send(grad.at[i, at(2, bottom(span))], rq_half.at[i, 0, land], s_sem.at[0], r_sem.at[0], q_up),
                send(grad.at[i, at(2, top(span))], rq_half.at[i, 1, land], s_sem.at[1], r_sem.at[1], q_down),
            )

    def start_terms(i):
        terms(i, 2)
        give_far(i, 0, 2, 3)
        start_halves(i, 0)
        terms(i, 0)
        give_far(i, 0, 1, 0)

    def start_rest(i):
        give_far(i, 1, 2)
        start_halves(i, 1)
        give_far(i, 1, 3, 1, 0)

    def pass_on(i, part):
        take_far(i, part, 1, 3)
        span = near(part, i)
        if span[1]:
            land, rest = slot_half(part, i), pl.ds(*span)
            s_sem, r_sem = sq_s.at[part, i], sq_r.at[part, i]
            up, down = halves[part, i]
            up.wait_recv()
            add_into(i, at(1, bottom(span)), rq_half.at[i, 0, land])
            a = send(grad.at[i, at(1, span)], rq.at[i, 0, rest], s_sem.at[2], r_sem.at[2], q_up)
            down.wait_recv()
            add_into(i, at(3, top(span)), rq_half.at[i, 1, land])
            b = send(grad.at[i, at(3, span)], rq.at[i, 1, rest], s_sem.at[3], r_sem.at[3], q_down)
            wholes[part, i] = a, b

    def settle(i, part):
        span = near(part, i)
        if not span[1]:
            return
        for copy in wholes[part, i]:
            copy.wait_recv()
        dp, dx = i // 2, i % 2
        rest = pl.ds(*span)
        own = at(0, span)
        land = slot_half(part, i)
        up, down = p_up, p_down
        if dx:
            add_into(i, own, rq.at[i, 0, rest], rq.at[i, 1, rest])
            sx[part, dp] = send(
                grad.at[i, own], rx.at[dp, rest], sx_s.at[part, dp], sx_r.at[part, dp], x_other
            )
        elif dp == 2:
            take_far(4, part, 0)
            add_into(i, own, rq.at[i, 0, rest], rq.at[i, 1, rest])
            crossed = near(part, 5)
            if crossed[1]:
                sx[part, 2].wait_recv()
                add_into(i, at(0, crossed), rx.at[2, pl.ds(*crossed)])
            p_half[part, 0] = send(
                grad.at[i, at(0, bottom(span))], rp_half.at[0, land], sp_s.at[part, 0], sp_r.at[part, 0], up
            )
            p_half[part, 1] = send(
                grad.at[i, at(0, top(span))], rp_half.at[1, land], sp_s.at[part, 1], sp_r.at[part, 1], down
            )
        elif dp:
            sx[part, dp].wait_recv()
            add_into(i, own, rq.at[i, 0, rest], rq.at[i, 1, rest], rx.at[dp, rest])
            k = dp // 2
            p_half[part, k].wait_recv()
            add_into(i, at(0, (bottom, top)[k](span)), rp_half.at[k, land])
            p_whole[part, k] = send(
                grad.at[i, own], rp.at[k, rest], sp_s.at[part, 2 + k], sp_r.at[part, 2 + k], (up, down)[k]
            )

    def step_rows(part):
        span = near(part, 0)
        rest = pl.ds(*span)
        for copy in wholes[part, 0]:
            copy.wait_recv()
        sx[part, 0].wait_recv()
        total = grad[0, at(0, span)].astype(F32)
        for term in (rq.at[0, 0], rq.at[0, 1], rx.at[0]):
            total = total + term[rest].astype(F32)
        for k in (1, 0):
            p_whole[part, k].wait_recv()
            total = total + rp[k, rest].astype(F32)
        stepped_out[rest] = rolled[rest] - total

    pad = rows_out.shape[1]
    part_width = vocab // 4
    exchange, spread = [], []

    def my_columns(who):
        return pl.ds(pl.multiple_of(who * part_width, part_width), part_width)

    def start_sync():
        step_rows(0)
        for k in range(4):
            rows_out[k] = stepped_out[pl.ds(0, pad), k * part_width : (k + 1) * part_width]
        for j, to in enumerate(siblings):
            exchange.append(send(rows_out.at[to[0]], rows_in.at[j], e_s.at[j], e_r.at[j], to))

    def turn_sync():
        held = roll_up(anchor[...])[:pad]
        summed = rows_out[r]
        for j, copy in enumerate(exchange):
            copy.wait_recv()
            summed = summed + rows_in[j]
        delta = held - summed / 4
        moment = 0.9 * roll_up(momentum[...])[:pad] + delta
        moment_out[...] = moment
        fresh_rows = held - 0.7 * (delta + 0.9 * moment)
        new_out[...] = fresh_rows
        for j, to in enumerate(siblings):
            spread.append(send(new_out, new_in.at[j], n_s.at[j], n_r.at[j], to))
        fresh_out[:, my_columns(r)] = fresh_rows

    def end_sync():
        for j, copy in enumerate(spread):
            copy.wait_recv()
            fresh_out[:, my_columns(siblings[j][0])] = new_in[j]

    act = {
        "T": start_terms,
        "h": start_rest,
        "P": lambda i: pass_on(i, 0),
        "S": lambda i: settle(i, 0),
        "p": lambda i: pass_on(i, 1),
        "s": lambda i: settle(i, 1),
        "X": lambda i: (start_sync, turn_sync, end_sync)[i](),
    }
    for step in PLAN:
        act[step[0]](int(step[1]))
    step_rows(1)
    for copy in sent:
        copy.wait_send()


def merge(
    loss, stepped, fresh, moment, momentum, step_index, frag_table, loss_out, weights_out, momentum_out, rolled
):
    frag_count = frag_table.shape[0]
    rows = stepped.shape[0]
    run = rows // frag_count
    pad = fresh.shape[0]
    pos = step_index[0] % frag_count
    frag = jnp.int32(0)
    for k in range(frag_count):
        frag = frag + jnp.where(pos == k, frag_table[k], 0)
    offset = pl.multiple_of(frag * run // 8 * 8, 8)
    skip = frag * run - offset

    def synced(shape):
        row = lax.broadcasted_iota(jnp.int32, shape, 0)
        return (row >= skip) & (row < skip + run)

    loss_out[...] = loss[...]
    mixed = jnp.where(synced(fresh.shape), fresh[...], stepped[pl.ds(0, pad)])
    for k in range(2):
        rolled[pl.ds(k * rows, pad)] = mixed
        rolled[pl.ds(k * rows + pad, rows - pad)] = stepped[pl.ds(pad, rows - pad)]
    weights_out[...] = rolled[pl.ds(pl.multiple_of((rows - offset) % rows, 8), rows)]
    momentum_out[...] = momentum[...]
    momentum_out[pl.ds(offset, pad)] = jnp.where(synced(moment.shape), moment[...], momentum[pl.ds(offset, pad)])


def on_device(tokens, targets, norm_gain, weights, anchor, momentum, step_index, frag_table):
    _, count, width = tokens.shape
    _, rows, vocab = weights.shape
    half = rows // 2
    part = vocab // 4
    run = rows // frag_table.shape[0]
    pad = -(-run // 8) * 8
    vmem = pl.BlockSpec(memory_space=pltpu.VMEM)
    smem = pl.BlockSpec(memory_space=pltpu.SMEM)
    dma = pltpu.SemaphoreType.DMA
    big = pltpu.VMEM((8, 4 * rows, vocab), BF16)
    shapes = (
        jax.ShapeDtypeStruct((1, count), F32),
        jax.ShapeDtypeStruct((rows, vocab), F32),
        jax.ShapeDtypeStruct((rows, part), F32),
    )
    loss, stepped, fresh, moment = pl.pallas_call(
        kernel,
        out_shape=shapes[:2] + (jax.ShapeDtypeStruct((pad, vocab), F32), jax.ShapeDtypeStruct((pad, part), F32)),
        in_specs=[pl.BlockSpec(memory_space=pl.ANY)] * 8,
        out_specs=(vmem,) * 4,
        scratch_shapes=[
            big,
            pltpu.VMEM((8, 4 * rows, count), BF16),
            big,
            pltpu.VMEM((vocab, count), F32),
            pltpu.VMEM((vocab, count), BF16),
            pltpu.VMEM((2, 128, width), BF16),
            pltpu.VMEM((8, 2, half, vocab), BF16),
            pltpu.VMEM((8, 2, rows, vocab), BF16),
            pltpu.VMEM((4, rows, vocab), BF16),
            pltpu.VMEM((4, rows - NEAR, vocab), BF16),
            pltpu.VMEM((2, half, vocab), BF16),
            pltpu.VMEM((2, rows, vocab), BF16),
            pltpu.VMEM((rows, vocab), F32),
            pltpu.VMEM((4, pad, part), F32),
            pltpu.VMEM((3, pad, part), F32),
            pltpu.VMEM((pad, part), F32),
            pltpu.VMEM((3, pad, part), F32),
            pltpu.VMEM((1, count), jnp.int32),
            pltpu.VMEM((1, width), F32),
            pltpu.VMEM((rows, vocab), F32),
            pltpu.VMEM((rows, part), F32),
            pltpu.VMEM((rows, part), F32),
            pltpu.SMEM(step_index.shape, jnp.int32),
            pltpu.SMEM(frag_table.shape, jnp.int32),
            dma((7,)),
            dma((2,)),
            dma((4,)), dma((4,)), dma((4,)), dma((4,)), dma((4,)), dma((4,)), dma((8, 4)), dma((8, 4)),
            dma((2, 4)), dma((2, 4)), dma((2, 4)), dma((2, 4)), dma((2, 4)), dma((2, 4)), dma((2, 8, 4)), dma((2, 8, 4)),
            dma((3,)), dma((3,)), dma((3,)), dma((3,)),
        ],
        compiler_params=pltpu.CompilerParams(
            collective_id=0, has_side_effects=True, vmem_limit_bytes=62 * 1024 * 1024
        ),
    )(
        tokens, targets, norm_gain[None], weights[0], anchor, momentum, step_index, frag_table
    )
    loss, weights_out, momentum_out = pl.pallas_call(
        merge, out_shape=shapes, in_specs=[vmem] * 5 + [smem] * 2, out_specs=(vmem,) * 3,
        scratch_shapes=[pltpu.VMEM((2 * rows, vocab), F32)],
    )(loss, stepped, fresh, moment, momentum, step_index, frag_table)
    return (loss, weights_out[None], momentum_out)


def solution(mesh):
    return jax.shard_map(
        on_device,
        mesh=mesh,
        in_specs=(
            P("rep", "fsdp", None),
            P("rep", "fsdp"),
            P(),
            P("rep", "fsdp", None),
            P("fsdp", "rep"),
            P("fsdp", "rep"),
            P(),
            P(),
        ),
        out_specs=(P("rep", "fsdp"), P("rep", "fsdp", None), P("fsdp", "rep")),
        check_vma=False,
    )
```

```python
import functools

import jax
import jax.numpy as jnp
import numpy as np
from jax import lax
from jax.experimental import pallas as pl
from jax.experimental.pallas import tpu as pltpu
from jax.sharding import PartitionSpec as P

F32 = jnp.float32
BF16 = jnp.bfloat16
MESH = pl.DeviceIdType.MESH

PLAN = (
    "T7", "h7", "T3", "P7", "h3", "T5", "h5", "p7",
    "T1", "p5", "h1", "T2", "h2", "T4", "p3", "T6",
    "P1", "T0", "P3", "S7", "P4", "h6", "P6", "S1",
    "h0", "P0", "S4", "s5", "P2", "p1", "h4", "S6",
    "S3", "s3", "p6", "S2", "s7", "p4", "X0", "p2",
    "s4", "s1", "p0", "X1", "s2", "s6", "X2",
)
FIRST = 32
ROLL = (16, 40, 80)
SLOT = (0, 1, 3, 2)
NEAR = 64


def dot(a, b, ca, cb):
    return lax.dot_general(a, b, (((ca,), (cb,)), ((), ())), preferred_element_type=F32)


def kernel(
    tokens, targets_in, gain_in, weights_in, anchor_in, momentum_in, step_in, table_in,
    loss_out, stepped_out, fresh_out, moment_out,
    head, normed_t, grad, logits_t, err_t, tok, rq_half, rq, rx, rx_far, rp_half, rp, rolled, rows_out, rows_in, new_out, new_in,
    targets, gain, weights, anchor, momentum, step_index, frag_table, load_sem, tok_sem, gp_s, gp_r, gx_s, gx_r, gf_s, gf_r, gq_s, gq_r,
    sp_s, sp_r, sx_s, sx_r, sf_s, sf_r, sq_s, sq_r, e_s, e_r, n_s, n_r,
):
    rows, vocab = weights.shape
    half = rows // 2
    count, width = tokens.shape[1:]
    frag_count = frag_table.shape[0]
    run = rows // frag_count
    chunk = tok.shape[1]
    scale = np.float32(1.0 / np.sqrt(np.float32(width)))

    r, f = lax.axis_index("rep"), lax.axis_index("fsdp")
    core = r % 2
    z, y, x = f // 8, (f // 2) % 4, f % 2
    p = jnp.where(core == 0, z, y)
    q = jnp.where(core == 0, y, z)

    def device(dp=0, dq=0, dx=0):
        pp, qq, xx = (p + dp) % 4, (q + dq) % 4, (x + dx) % 2
        return (r, jnp.where(core == 0, pp, qq) * 8 + jnp.where(core == 0, qq, pp) * 2 + xx)

    p_up, p_down, q_up, q_down, x_other = device(dp=1), device(dp=3), device(dq=1), device(dq=3), device(dx=1)

    def sibling(j):
        c2, l2 = (core + j) % 2, (r // 2 + j // 2) % 2
        return l2 * 2 + c2

    siblings = [(sibling(j), f) for j in (1, 2, 3)]

    barrier = pltpu.get_barrier_semaphore()
    partners = [p_up, p_down, q_up, q_down, x_other] + siblings
    for partner in partners:
        pl.semaphore_signal(barrier, inc=1, device_id=partner, device_id_type=MESH)

    chunks = count // chunk
    slots = tok.shape[0]

    def token_copy(c):
        return pltpu.make_async_copy(
            tokens.at[0, pl.ds(c * chunk, chunk)], tok.at[c % slots], tok_sem.at[c % slots]
        )

    pairs = (
        (step_in, step_index), (table_in, frag_table), (weights_in, weights), (gain_in, gain),
        (targets_in, targets), (anchor_in, anchor), (momentum_in, momentum),
    )
    loads = [pltpu.make_async_copy(src, dst, load_sem.at[k]) for k, (src, dst) in enumerate(pairs)]
    for load in loads[:3]:
        load.start()
    for c in range(slots):
        token_copy(c).start()
    for load in loads[3:]:
        load.start()
    for load in loads[:3]:
        load.wait()
    pos = step_index[0] % frag_count
    frag = jnp.int32(0)
    for k in range(frag_count):
        frag = frag + jnp.where(pos == k, frag_table[k], 0)
    bits = [frag % 2 == 1, frag // 2 % 2 == 1, frag // 4 == 1]

    def roll_up(value):
        for bit, step in zip(bits, ROLL):
            value = jnp.where(bit, jnp.concatenate([value[step:], value[:step]]), value)
        return value

    rolled[...] = roll_up(weights[...])
    head[0, pl.ds(0, rows)] = rolled[...].astype(BF16)
    pl.semaphore_wait(barrier, len(partners))

    sent = []

    def send(src, dst, s_sem, r_sem, to):
        copy = pltpu.make_async_remote_copy(
            src_ref=src, dst_ref=dst, send_sem=s_sem, recv_sem=r_sem, device_id=to, device_id_type=MESH
        )
        copy.start()
        sent.append(copy)
        return copy

    def whole(dq, i=0):
        return pl.ds(SLOT[dq] * rows, NEAR if i == 5 else rows)

    def low(dq, i=0):
        return pl.ds(SLOT[dq] * rows, NEAR // 2 if i == 5 else half)

    def high(dq, i=0):
        cut = NEAR // 2 if i == 5 else half
        return pl.ds(SLOT[dq] * rows + cut, cut)

    def far(dq):
        return pl.ds(SLOT[dq] * rows + NEAR, rows - NEAR)

    def gather_q(i):
        a = send(head.at[i, whole(0, i)], head.at[i, whole(3, i)], gq_s.at[i, 0], gq_r.at[i, 0], q_up)
        b = send(head.at[i, whole(0, i)], head.at[i, whole(1, i)], gq_s.at[i, 1], gq_r.at[i, 1], q_down)
        return a, b

    def forward_q(i, pair):
        pair[0].wait_recv()
        a = send(head.at[i, low(3, i)], head.at[i, low(2, i)], gq_s.at[i, 2], gq_r.at[i, 2], q_up)
        pair[1].wait_recv()
        b = send(head.at[i, high(1, i)], head.at[i, high(2, i)], gq_s.at[i, 3], gq_r.at[i, 3], q_down)
        return a, b

    def gather_x(dp):
        i = 2 * dp
        return send(head.at[i, whole(0, i + 1)], head.at[i + 1, whole(0, i + 1)], gx_s.at[dp], gx_r.at[dp], x_other)

    def gather_far(dq):
        return send(head.at[4, far(dq)], head.at[5, far(dq)], gf_s.at[dq], gf_r.at[dq], x_other)

    def norm_chunk(c, slot):
        xf = tok[slot].astype(F32)
        inv = lax.rsqrt(jnp.sum(xf * xf, axis=1, keepdims=True) * np.float32(1.0 / width) + np.float32(1e-5))

        def unit(j, carry):
            columns = pl.ds(pl.multiple_of(j * 4 * rows, 128), 4 * rows)
            part = (tok[slot, :, columns].astype(F32) * inv * gain[:, columns]).T
            for b in range(4):
                bz, by, bx = j // 2, 2 * (j % 2) + b // 2, b % 2
                dp = (jnp.where(core == 0, bz, by) - p + 4) % 4
                dq = (jnp.where(core == 0, by, bz) - q + 4) % 4
                dx = (bx + x) % 2
                normed_t[
                    2 * dp + dx,
                    pl.ds(pl.multiple_of((dq ^ (dq >> 1)) * rows, 16), rows),
                    pl.ds(pl.multiple_of(c * chunk, chunk), chunk),
                ] = roll_up(part[b * rows : (b + 1) * rows]).astype(BF16)
            return carry

        lax.fori_loop(0, width // (4 * rows), unit, 0)

    def norm(first, last):
        for c in range(first, last):
            token_copy(c).wait()
            norm_chunk(c, c % slots)
            if c + slots < chunks:
                token_copy(c + slots).start()

    early = pl.ds(0, 3 * rows)
    last = pl.ds(3 * rows, rows)

    def add_logits(i, where=pl.ds(0, 4 * rows), fresh=False):
        tile = vocab // 2

        def step(j, carry):
            s = pl.ds(pl.multiple_of(j * tile, tile), tile)
            term = dot(head[i, where, s], normed_t[i, where], 0, 0)
            if fresh:
                logits_t[s, :] = term
            else:
                logits_t[s, :] += term
            return carry

        lax.fori_loop(0, vocab // tile, step, 0)

    def settle_q(i):
        fq[i][0].wait_recv()
        fq[i][1].wait_recv()

    def finish(i, fresh=False):
        settle_q(i)
        add_logits(i, fresh=fresh)

    own = head.at[0, whole(0)]
    up = send(own, head.at[6, whole(0)], gp_s.at[0], gp_r.at[0], p_up)
    down = send(own, head.at[2, whole(0)], gp_s.at[1], gp_r.at[1], p_down)
    gx, gq, fq, gf = {0: gather_x(0)}, {0: gather_q(0)}, {}, {}
    for load in loads[3:]:
        load.wait()
    norm(0, 4)
    up.wait_recv()
    up2 = send(head.at[6, low(0)], head.at[4, low(0)], gp_s.at[2], gp_r.at[2], p_up)
    down.wait_recv()
    down2 = send(head.at[2, high(0)], head.at[4, high(0)], gp_s.at[3], gp_r.at[3], p_down)
    gx[1] = gather_x(1)
    gx[3] = gather_x(3)
    gq[2] = gather_q(2)
    gq[6] = gather_q(6)
    norm(4, 6)
    fq[0] = forward_q(0, gq[0])
    up2.wait_recv()
    down2.wait_recv()
    gq[4] = gather_q(4)
    gx[2] = gather_x(2)
    gf[0] = gather_far(0)
    gx[0].wait_recv()
    gq[1] = gather_q(1)
    norm(6, 8)
    fq[2] = forward_q(2, gq[2])
    fq[6] = forward_q(6, gq[6])
    finish(0, fresh=True)
    fq[4] = forward_q(4, gq[4])
    gf[1] = gather_far(1)
    gf[3] = gather_far(3)
    gx[1].wait_recv()
    gq[3] = gather_q(3)
    finish(2)
    fq[4][0].wait_recv()
    fq[4][1].wait_recv()
    gf[2] = gather_far(2)
    gx[3].wait_recv()
    gq[7] = gather_q(7)
    fq[1] = forward_q(1, gq[1])
    finish(6)
    gx[2].wait_recv()
    gq[5] = gather_q(5)
    fq[3] = forward_q(3, gq[3])
    add_logits(4)
    fq[7] = forward_q(7, gq[7])
    finish(1)
    fq[5] = forward_q(5, gq[5])
    add_logits(3, early)
    add_logits(7, early)
    for dq in (0, 1, 3):
        gf[dq].wait_recv()
    add_logits(5, early)
    gf[2].wait_recv()
    tail = (3, 7, 5)
    for i in tail:
        settle_q(i)

    lanes = 128

    def soften(j, carry):
        s = pl.ds(j * lanes, lanes)
        logit = logits_t[:, s] * scale
        expo = jnp.exp(logit)
        total = jnp.sum(expo, axis=0, keepdims=True)
        onehot = lax.broadcasted_iota(jnp.int32, (vocab, lanes), 0) == targets[:, s]
        picked = jnp.sum(jnp.where(onehot, logit, 0.0), axis=0, keepdims=True)
        loss_out[:, s] = jnp.log(total) - picked
        err_t[:, s] = (expo * (1.0 / total) - jnp.where(onehot, 1.0, 0.0)).astype(BF16)
        return carry

    late_head = jnp.concatenate([head[i, last] for i in tail])
    parts = 2
    for k in range(parts):
        s = pl.ds(k * count // parts, count // parts)
        late_tokens = jnp.concatenate([normed_t[i, last, s] for i in tail])
        logits_t[:, s] += dot(late_head, late_tokens, 0, 0)
        for j in range(count // parts // lanes):
            soften(k * (count // parts // lanes) + j, 0)

    def terms(i, slot):
        two = pl.ds(slot * rows, 2 * rows)
        grad[i, two] = (dot(normed_t[i, two], err_t[...], 1, 1) * scale).astype(BF16)

    def add_into(i, where, *others):
        total = grad[i, where].astype(F32)
        for other in others:
            total = total + other[...].astype(F32)
        grad[i, where] = total.astype(BF16)

    def near(part, i):
        if i == 5:
            return (0, 0) if part == 0 else (FIRST, NEAR)
        return (0, FIRST) if part == 0 else (FIRST, rows - FIRST)

    def beyond(part):
        return (0, FIRST) if part == 0 else (FIRST + NEAR, rows - FIRST - NEAR)

    def at(dq, span):
        return pl.ds(SLOT[dq] * rows + span[0], span[1])

    def bottom(span):
        return span[0], span[1] // 2

    def top(span):
        return span[0] + span[1] // 2, span[1] // 2

    def slot_half(part, i):
        return pl.ds(0 if part == 0 else FIRST // 2, near(part, i)[1] // 2)

    def slot_far(part):
        return pl.ds(0 if part == 0 else FIRST, beyond(part)[1])

    sf, sx, p_half, p_whole, halves, wholes = {}, {}, {}, {}, {}, {}

    def take_far(i, part, *offsets):
        for dq in offsets if i == 4 else ():
            sf[part, dq].wait_recv()
            add_into(4, at(dq, beyond(part)), rx_far.at[dq, slot_far(part)])

    def give_far(i, part, *offsets):
        for dq in offsets if i == 5 else ():
            sf[part, dq] = send(
                grad.at[5, at(dq, beyond(part))], rx_far.at[dq, slot_far(part)],
                sf_s.at[part, dq], sf_r.at[part, dq], x_other,
            )

    def start_halves(i, part):
        take_far(i, part, 2)
        span = near(part, i)
        if span[1]:
            land = slot_half(part, i)
            s_sem, r_sem = sq_s.at[part, i], sq_r.at[part, i]
            halves[part, i] = (
                send(grad.at[i, at(2, bottom(span))], rq_half.at[i, 0, land], s_sem.at[0], r_sem.at[0], q_up),
                send(grad.at[i, at(2, top(span))], rq_half.at[i, 1, land], s_sem.at[1], r_sem.at[1], q_down),
            )

    def start_terms(i):
        terms(i, 2)
        give_far(i, 0, 2, 3)
        start_halves(i, 0)
        terms(i, 0)
        give_far(i, 0, 1, 0)

    def start_rest(i):
        give_far(i, 1, 2)
        start_halves(i, 1)
        give_far(i, 1, 3, 1, 0)

    def pass_on(i, part):
        take_far(i, part, 1, 3)
        span = near(part, i)
        if span[1]:
            land, rest = slot_half(part, i), pl.ds(*span)
            s_sem, r_sem = sq_s.at[part, i], sq_r.at[part, i]
            up, down = halves[part, i]
            up.wait_recv()
            add_into(i, at(1, bottom(span)), rq_half.at[i, 0, land])
            a = send(grad.at[i, at(1, span)], rq.at[i, 0, rest], s_sem.at[2], r_sem.at[2], q_up)
            down.wait_recv()
            add_into(i, at(3, top(span)), rq_half.at[i, 1, land])
            b = send(grad.at[i, at(3, span)], rq.at[i, 1, rest], s_sem.at[3], r_sem.at[3], q_down)
            wholes[part, i] = a, b

    def settle(i, part):
        span = near(part, i)
        if not span[1]:
            return
        for copy in wholes[part, i]:
            copy.wait_recv()
        dp, dx = i // 2, i % 2
        rest = pl.ds(*span)
        own = at(0, span)
        land = slot_half(part, i)
        up, down = p_up, p_down
        if dx:
            add_into(i, own, rq.at[i, 0, rest], rq.at[i, 1, rest])
            sx[part, dp] = send(
                grad.at[i, own], rx.at[dp, rest], sx_s.at[part, dp], sx_r.at[part, dp], x_other
            )
        elif dp == 2:
            take_far(4, part, 0)
            add_into(i, own, rq.at[i, 0, rest], rq.at[i, 1, rest])
            crossed = near(part, 5)
            if crossed[1]:
                sx[part, 2].wait_recv()
                add_into(i, at(0, crossed), rx.at[2, pl.ds(*crossed)])
            p_half[part, 0] = send(
                grad.at[i, at(0, bottom(span))], rp_half.at[0, land], sp_s.at[part, 0], sp_r.at[part, 0], up
            )
            p_half[part, 1] = send(
                grad.at[i, at(0, top(span))], rp_half.at[1, land], sp_s.at[part, 1], sp_r.at[part, 1], down
            )
        elif dp:
            sx[part, dp].wait_recv()
            add_into(i, own, rq.at[i, 0, rest], rq.at[i, 1, rest], rx.at[dp, rest])
            k = dp // 2
            p_half[part, k].wait_recv()
            add_into(i, at(0, (bottom, top)[k](span)), rp_half.at[k, land])
            p_whole[part, k] = send(
                grad.at[i, own], rp.at[k, rest], sp_s.at[part, 2 + k], sp_r.at[part, 2 + k], (up, down)[k]
            )

    def step_rows(part):
        span = near(part, 0)
        rest = pl.ds(*span)
        for copy in wholes[part, 0]:
            copy.wait_recv()
        sx[part, 0].wait_recv()
        total = grad[0, at(0, span)].astype(F32)
        for term in (rq.at[0, 0], rq.at[0, 1], rx.at[0]):
            total = total + term[rest].astype(F32)
        for k in (1, 0):
            p_whole[part, k].wait_recv()
            total = total + rp[k, rest].astype(F32)
        stepped_out[rest] = rolled[rest] - total

    pad = rows_out.shape[1]
    part_width = vocab // 4
    exchange, spread = [], []

    def my_columns(who):
        return pl.ds(pl.multiple_of(who * part_width, part_width), part_width)

    def start_sync():
        step_rows(0)
        for k in range(4):
            rows_out[k] = stepped_out[pl.ds(0, pad), k * part_width : (k + 1) * part_width]
        for j, to in enumerate(siblings):
            exchange.append(send(rows_out.at[to[0]], rows_in.at[j], e_s.at[j], e_r.at[j], to))

    def turn_sync():
        held = roll_up(anchor[...])[:pad]
        summed = rows_out[r]
        for j, copy in enumerate(exchange):
            copy.wait_recv()
            summed = summed + rows_in[j]
        delta = held - summed / 4
        moment = 0.9 * roll_up(momentum[...])[:pad] + delta
        moment_out[...] = moment
        fresh_rows = held - 0.7 * (delta + 0.9 * moment)
        new_out[...] = fresh_rows
        for j, to in enumerate(siblings):
            spread.append(send(new_out, new_in.at[j], n_s.at[j], n_r.at[j], to))
        fresh_out[:, my_columns(r)] = fresh_rows

    def end_sync():
        for j, copy in enumerate(spread):
            copy.wait_recv()
            fresh_out[:, my_columns(siblings[j][0])] = new_in[j]

    act = {
        "T": start_terms,
        "h": start_rest,
        "P": lambda i: pass_on(i, 0),
        "S": lambda i: settle(i, 0),
        "p": lambda i: pass_on(i, 1),
        "s": lambda i: settle(i, 1),
        "X": lambda i: (start_sync, turn_sync, end_sync)[i](),
    }
    for step in PLAN:
        act[step[0]](int(step[1]))
    step_rows(1)
    for copy in sent:
        copy.wait_send()


def merge(
    loss, stepped, fresh, moment, momentum, step_index, frag_table, loss_out, weights_out, momentum_out, rolled
):
    frag_count = frag_table.shape[0]
    rows = stepped.shape[0]
    run = rows // frag_count
    pad = fresh.shape[0]
    pos = step_index[0] % frag_count
    frag = jnp.int32(0)
    for k in range(frag_count):
        frag = frag + jnp.where(pos == k, frag_table[k], 0)
    offset = pl.multiple_of(frag * run // 8 * 8, 8)
    skip = frag * run - offset

    def synced(shape):
        row = lax.broadcasted_iota(jnp.int32, shape, 0)
        return (row >= skip) & (row < skip + run)

    loss_out[...] = loss[...]
    mixed = jnp.where(synced(fresh.shape), fresh[...], stepped[pl.ds(0, pad)])
    for k in range(2):
        rolled[pl.ds(k * rows, pad)] = mixed
        rolled[pl.ds(k * rows + pad, rows - pad)] = stepped[pl.ds(pad, rows - pad)]
    weights_out[...] = rolled[pl.ds(pl.multiple_of((rows - offset) % rows, 8), rows)]
    momentum_out[...] = momentum[...]
    momentum_out[pl.ds(offset, pad)] = jnp.where(synced(moment.shape), moment[...], momentum[pl.ds(offset, pad)])


def on_device(tokens, targets, norm_gain, weights, anchor, momentum, step_index, frag_table):
    _, count, width = tokens.shape
    _, rows, vocab = weights.shape
    half = rows // 2
    part = vocab // 4
    run = rows // frag_table.shape[0]
    pad = -(-run // 8) * 8
    vmem = pl.BlockSpec(memory_space=pltpu.VMEM)
    smem = pl.BlockSpec(memory_space=pltpu.SMEM)
    dma = pltpu.SemaphoreType.DMA
    big = pltpu.VMEM((8, 4 * rows, vocab), BF16)
    shapes = (
        jax.ShapeDtypeStruct((1, count), F32),
        jax.ShapeDtypeStruct((rows, vocab), F32),
        jax.ShapeDtypeStruct((rows, part), F32),
    )
    loss, stepped, fresh, moment = pl.pallas_call(
        kernel,
        out_shape=shapes[:2] + (jax.ShapeDtypeStruct((pad, vocab), F32), jax.ShapeDtypeStruct((pad, part), F32)),
        in_specs=[pl.BlockSpec(memory_space=pl.ANY)] * 8,
        out_specs=(vmem,) * 4,
        scratch_shapes=[
            big,
            pltpu.VMEM((8, 4 * rows, count), BF16),
            big,
            pltpu.VMEM((vocab, count), F32),
            pltpu.VMEM((vocab, count), BF16),
            pltpu.VMEM((2, 128, width), BF16),
            pltpu.VMEM((8, 2, half, vocab), BF16),
            pltpu.VMEM((8, 2, rows, vocab), BF16),
            pltpu.VMEM((4, rows, vocab), BF16),
            pltpu.VMEM((4, rows - NEAR, vocab), BF16),
            pltpu.VMEM((2, half, vocab), BF16),
            pltpu.VMEM((2, rows, vocab), BF16),
            pltpu.VMEM((rows, vocab), F32),
            pltpu.VMEM((4, pad, part), F32),
            pltpu.VMEM((3, pad, part), F32),
            pltpu.VMEM((pad, part), F32),
            pltpu.VMEM((3, pad, part), F32),
            pltpu.VMEM((1, count), jnp.int32),
            pltpu.VMEM((1, width), F32),
            pltpu.VMEM((rows, vocab), F32),
            pltpu.VMEM((rows, part), F32),
            pltpu.VMEM((rows, part), F32),
            pltpu.SMEM(step_index.shape, jnp.int32),
            pltpu.SMEM(frag_table.shape, jnp.int32),
            dma((7,)),
            dma((2,)),
            dma((4,)), dma((4,)), dma((4,)), dma((4,)), dma((4,)), dma((4,)), dma((8, 4)), dma((8, 4)),
            dma((2, 4)), dma((2, 4)), dma((2, 4)), dma((2, 4)), dma((2, 4)), dma((2, 4)), dma((2, 8, 4)), dma((2, 8, 4)),
            dma((3,)), dma((3,)), dma((3,)), dma((3,)),
        ],
        compiler_params=pltpu.CompilerParams(
            collective_id=0, has_side_effects=True, vmem_limit_bytes=62 * 1024 * 1024
        ),
    )(
        tokens, targets, norm_gain[None], weights[0], anchor, momentum, step_index, frag_table
    )
    loss, weights_out, momentum_out = pl.pallas_call(
        merge, out_shape=shapes, in_specs=[vmem] * 5 + [smem] * 2, out_specs=(vmem,) * 3,
        scratch_shapes=[pltpu.VMEM((2 * rows, vocab), F32)],
    )(loss, stepped, fresh, moment, momentum, step_index, frag_table)
    return (loss, weights_out[None], momentum_out)


def solution(mesh):
    return jax.shard_map(
        on_device,
        mesh=mesh,
        in_specs=(
            P("rep", "fsdp", None),
            P("rep", "fsdp"),
            P(),
            P("rep", "fsdp", None),
            P("fsdp", "rep"),
            P("fsdp", "rep"),
            P(),
            P(),
        ),
        out_specs=(P("rep", "fsdp"), P("rep", "fsdp", None), P("fsdp", "rep")),
        check_vma=False,
    )
```

```python
import functools

import jax
import jax.numpy as jnp
import numpy as np
from jax import lax
from jax.experimental import pallas as pl
from jax.experimental.pallas import tpu as pltpu
from jax.sharding import PartitionSpec as P

F32 = jnp.float32
BF16 = jnp.bfloat16
MESH = pl.DeviceIdType.MESH

PLAN = (
    "Z7", "T3", "P7", "h3", "T5", "h5", "p7",
    "T1", "p5", "h1", "T2", "h2", "T4", "p3", "T6",
    "P1", "T0", "P3", "S7", "P4", "h6", "P6", "S1",
    "h0", "P0", "S4", "s5", "P2", "p1", "h4", "S6",
    "S3", "s3", "p6", "S2", "s7", "p4", "X0", "p2",
    "s4", "s1", "p0", "X1", "s2", "s6", "X2",
)
FIRST = 32
ROLL = (16, 40, 80)
SLOT = (0, 1, 3, 2)
NEAR = 64


def dot(a, b, ca, cb):
    return lax.dot_general(a, b, (((ca,), (cb,)), ((), ())), preferred_element_type=F32)


def kernel(
    tokens, targets_in, gain_in, weights_in, anchor_in, momentum_in, step_in, table_in,
    loss_out, stepped_out, fresh_out, moment_out,
    head, normed_t, grad, logits_t, err_t, tok, rq_half, rq, rx, rx_far, rp_half, rp, rolled, rows_out, rows_in, new_out, new_in,
    targets, gain, weights, anchor, momentum, step_index, frag_table, load_sem, tok_sem, gp_s, gp_r, gx_s, gx_r, gf_s, gf_r, gq_s, gq_r,
    sp_s, sp_r, sx_s, sx_r, sf_s, sf_r, sq_s, sq_r, e_s, e_r, n_s, n_r,
):
    rows, vocab = weights.shape
    half = rows // 2
    count, width = tokens.shape[1:]
    frag_count = frag_table.shape[0]
    run = rows // frag_count
    chunk = tok.shape[1]
    scale = np.float32(1.0 / np.sqrt(np.float32(width)))

    r, f = lax.axis_index("rep"), lax.axis_index("fsdp")
    core = r % 2
    z, y, x = f // 8, (f // 2) % 4, f % 2
    p = jnp.where(core == 0, z, y)
    q = jnp.where(core == 0, y, z)

    def device(dp=0, dq=0, dx=0):
        pp, qq, xx = (p + dp) % 4, (q + dq) % 4, (x + dx) % 2
        return (r, jnp.where(core == 0, pp, qq) * 8 + jnp.where(core == 0, qq, pp) * 2 + xx)

    p_up, p_down, q_up, q_down, x_other = device(dp=1), device(dp=3), device(dq=1), device(dq=3), device(dx=1)

    def sibling(j):
        c2, l2 = (core + j) % 2, (r // 2 + j // 2) % 2
        return l2 * 2 + c2

    siblings = [(sibling(j), f) for j in (1, 2, 3)]

    barrier = pltpu.get_barrier_semaphore()
    partners = [p_up, p_down, q_up, q_down, x_other] + siblings
    for partner in partners:
        pl.semaphore_signal(barrier, inc=1, device_id=partner, device_id_type=MESH)

    chunks = count // chunk
    slots = tok.shape[0]

    def token_copy(c):
        return pltpu.make_async_copy(
            tokens.at[0, pl.ds(c * chunk, chunk)], tok.at[c % slots], tok_sem.at[c % slots]
        )

    pairs = (
        (step_in, step_index), (table_in, frag_table), (weights_in, weights), (gain_in, gain),
        (targets_in, targets), (anchor_in, anchor), (momentum_in, momentum),
    )
    loads = [pltpu.make_async_copy(src, dst, load_sem.at[k]) for k, (src, dst) in enumerate(pairs)]
    for load in loads[:3]:
        load.start()
    for c in range(slots):
        token_copy(c).start()
    for load in loads[3:]:
        load.start()
    for load in loads[:3]:
        load.wait()
    pos = step_index[0] % frag_count
    frag = jnp.int32(0)
    for k in range(frag_count):
        frag = frag + jnp.where(pos == k, frag_table[k], 0)
    bits = [frag % 2 == 1, frag // 2 % 2 == 1, frag // 4 == 1]

    def roll_up(value):
        for bit, step in zip(bits, ROLL):
            value = jnp.where(bit, jnp.concatenate([value[step:], value[:step]]), value)
        return value

    rolled[...] = roll_up(weights[...])
    head[0, pl.ds(0, rows)] = rolled[...].astype(BF16)
    pl.semaphore_wait(barrier, len(partners))

    sent = []

    def send(src, dst, s_sem, r_sem, to):
        copy = pltpu.make_async_remote_copy(
            src_ref=src, dst_ref=dst, send_sem=s_sem, recv_sem=r_sem, device_id=to, device_id_type=MESH
        )
        copy.start()
        sent.append(copy)
        return copy

    def whole(dq, i=0):
        return pl.ds(SLOT[dq] * rows, NEAR if i == 5 else rows)

    def low(dq, i=0):
        return pl.ds(SLOT[dq] * rows, NEAR // 2 if i == 5 else half)

    def high(dq, i=0):
        cut = NEAR // 2 if i == 5 else half
        return pl.ds(SLOT[dq] * rows + cut, cut)

    def far(dq):
        return pl.ds(SLOT[dq] * rows + NEAR, rows - NEAR)

    def gather_q(i):
        a = send(head.at[i, whole(0, i)], head.at[i, whole(3, i)], gq_s.at[i, 0], gq_r.at[i, 0], q_up)
        b = send(head.at[i, whole(0, i)], head.at[i, whole(1, i)], gq_s.at[i, 1], gq_r.at[i, 1], q_down)
        return a, b

    def forward_q(i, pair):
        pair[0].wait_recv()
        a = send(head.at[i, low(3, i)], head.at[i, low(2, i)], gq_s.at[i, 2], gq_r.at[i, 2], q_up)
        pair[1].wait_recv()
        b = send(head.at[i, high(1, i)], head.at[i, high(2, i)], gq_s.at[i, 3], gq_r.at[i, 3], q_down)
        return a, b

    def gather_x(dp):
        i = 2 * dp
        return send(head.at[i, whole(0, i + 1)], head.at[i + 1, whole(0, i + 1)], gx_s.at[dp], gx_r.at[dp], x_other)

    def gather_far(dq):
        return send(head.at[4, far(dq)], head.at[5, far(dq)], gf_s.at[dq], gf_r.at[dq], x_other)

    def norm_chunk(c, slot):
        xf = tok[slot].astype(F32)
        inv = lax.rsqrt(jnp.sum(xf * xf, axis=1, keepdims=True) * np.float32(1.0 / width) + np.float32(1e-5))

        def unit(j, carry):
            columns = pl.ds(pl.multiple_of(j * 4 * rows, 128), 4 * rows)
            part = (tok[slot, :, columns].astype(F32) * inv * gain[:, columns]).T
            for b in range(4):
                bz, by, bx = j // 2, 2 * (j % 2) + b // 2, b % 2
                dp = (jnp.where(core == 0, bz, by) - p + 4) % 4
                dq = (jnp.where(core == 0, by, bz) - q + 4) % 4
                dx = (bx + x) % 2
                normed_t[
                    2 * dp + dx,
                    pl.ds(pl.multiple_of((dq ^ (dq >> 1)) * rows, 16), rows),
                    pl.ds(pl.multiple_of(c * chunk, chunk), chunk),
                ] = roll_up(part[b * rows : (b + 1) * rows]).astype(BF16)
            return carry

        lax.fori_loop(0, width // (4 * rows), unit, 0)

    def norm(first, last):
        for c in range(first, last):
            token_copy(c).wait()
            norm_chunk(c, c % slots)
            if c + slots < chunks:
                token_copy(c + slots).start()

    early = pl.ds(0, 3 * rows)
    last = pl.ds(3 * rows, rows)

    def add_logits(i, where=pl.ds(0, 4 * rows), fresh=False):
        tile = vocab // 2

        def step(j, carry):
            s = pl.ds(pl.multiple_of(j * tile, tile), tile)
            term = dot(head[i, where, s], normed_t[i, where], 0, 0)
            if fresh:
                logits_t[s, :] = term
            else:
                logits_t[s, :] += term
            return carry

        lax.fori_loop(0, vocab // tile, step, 0)

    def settle_q(i):
        fq[i][0].wait_recv()
        fq[i][1].wait_recv()

    def finish(i, fresh=False):
        settle_q(i)
        add_logits(i, fresh=fresh)

    own = head.at[0, whole(0)]
    up = send(own, head.at[6, whole(0)], gp_s.at[0], gp_r.at[0], p_up)
    down = send(own, head.at[2, whole(0)], gp_s.at[1], gp_r.at[1], p_down)
    gx, gq, fq, gf = {0: gather_x(0)}, {0: gather_q(0)}, {}, {}
    for load in loads[3:]:
        load.wait()
    norm(0, 4)
    up.wait_recv()
    up2 = send(head.at[6, low(0)], head.at[4, low(0)], gp_s.at[2], gp_r.at[2], p_up)
    down.wait_recv()
    down2 = send(head.at[2, high(0)], head.at[4, high(0)], gp_s.at[3], gp_r.at[3], p_down)
    gx[1] = gather_x(1)
    gx[3] = gather_x(3)
    gq[2] = gather_q(2)
    gq[6] = gather_q(6)
    norm(4, 6)
    fq[0] = forward_q(0, gq[0])
    up2.wait_recv()
    down2.wait_recv()
    gq[4] = gather_q(4)
    gx[2] = gather_x(2)
    gf[0] = gather_far(0)
    gx[0].wait_recv()
    gq[1] = gather_q(1)
    norm(6, 8)
    fq[2] = forward_q(2, gq[2])
    fq[6] = forward_q(6, gq[6])
    finish(0, fresh=True)
    fq[4] = forward_q(4, gq[4])
    gf[1] = gather_far(1)
    gf[3] = gather_far(3)
    gx[1].wait_recv()
    gq[3] = gather_q(3)
    finish(2)
    fq[4][0].wait_recv()
    fq[4][1].wait_recv()
    gf[2] = gather_far(2)
    gx[3].wait_recv()
    gq[7] = gather_q(7)
    fq[1] = forward_q(1, gq[1])
    finish(6)
    gx[2].wait_recv()
    gq[5] = gather_q(5)
    fq[3] = forward_q(3, gq[3])
    add_logits(4)
    fq[7] = forward_q(7, gq[7])
    finish(1)
    fq[5] = forward_q(5, gq[5])
    add_logits(3, early)
    add_logits(7, early)
    for dq in (0, 1, 3):
        gf[dq].wait_recv()
    add_logits(5, early)
    gf[2].wait_recv()
    tail = (3, 7, 5)
    for i in tail:
        settle_q(i)

    lanes = 128

    def soften(j, carry):
        s = pl.ds(j * lanes, lanes)
        raw = logits_t[:, s]
        expo = jnp.exp2(raw * np.float32(scale / np.log(2.0)))
        total = jnp.sum(expo, axis=0, keepdims=True)
        onehot = lax.broadcasted_iota(jnp.int32, (vocab, lanes), 0) == targets[:, s]
        picked = jnp.sum(jnp.where(onehot, raw, 0.0), axis=0, keepdims=True) * scale
        loss_out[:, s] = jnp.log(total) - picked
        err_t[:, s] = (expo * (1.0 / total) - jnp.where(onehot, 1.0, 0.0)).astype(BF16)
        return carry

    late_head = jnp.concatenate([head[i, last] for i in tail])
    parts = 2
    for k in range(parts):
        s = pl.ds(k * count // parts, count // parts)
        late_tokens = jnp.concatenate([normed_t[i, last, s] for i in tail])
        logits_t[:, s] += dot(late_head, late_tokens, 0, 0)
        for j in range(count // parts // lanes):
            soften(k * (count // parts // lanes) + j, 0)

    def terms(i, slot):
        two = pl.ds(slot * rows, 2 * rows)
        grad[i, two] = (dot(normed_t[i, two], err_t[...], 1, 1) * scale).astype(BF16)

    def add_into(i, where, *others):
        total = grad[i, where].astype(F32)
        for other in others:
            total = total + other[...].astype(F32)
        grad[i, where] = total.astype(BF16)

    def near(part, i):
        if i == 5:
            return (0, 0) if part == 0 else (FIRST, NEAR)
        return (0, FIRST) if part == 0 else (FIRST, rows - FIRST)

    def beyond(part):
        return (0, FIRST) if part == 0 else (FIRST + NEAR, rows - FIRST - NEAR)

    def at(dq, span):
        return pl.ds(SLOT[dq] * rows + span[0], span[1])

    def bottom(span):
        return span[0], span[1] // 2

    def top(span):
        return span[0] + span[1] // 2, span[1] // 2

    def slot_half(part, i):
        return pl.ds(0 if part == 0 else FIRST // 2, near(part, i)[1] // 2)

    def slot_far(part):
        return pl.ds(0 if part == 0 else FIRST, beyond(part)[1])

    sf, sx, p_half, p_whole, halves, wholes = {}, {}, {}, {}, {}, {}

    def take_far(i, part, *offsets):
        for dq in offsets if i == 4 else ():
            sf[part, dq].wait_recv()
            add_into(4, at(dq, beyond(part)), rx_far.at[dq, slot_far(part)])

    def give_far(i, part, *offsets):
        for dq in offsets if i == 5 else ():
            sf[part, dq] = send(
                grad.at[5, at(dq, beyond(part))], rx_far.at[dq, slot_far(part)],
                sf_s.at[part, dq], sf_r.at[part, dq], x_other,
            )

    def start_halves(i, part):
        take_far(i, part, 2)
        span = near(part, i)
        if span[1]:
            land = slot_half(part, i)
            s_sem, r_sem = sq_s.at[part, i], sq_r.at[part, i]
            halves[part, i] = (
                send(grad.at[i, at(2, bottom(span))], rq_half.at[i, 0, land], s_sem.at[0], r_sem.at[0], q_up),
                send(grad.at[i, at(2, top(span))], rq_half.at[i, 1, land], s_sem.at[1], r_sem.at[1], q_down),
            )

    def start_terms(i):
        terms(i, 2)
        give_far(i, 0, 2, 3)
        start_halves(i, 0)
        terms(i, 0)
        give_far(i, 0, 1, 0)

    def start_both(i):
        terms(i, 2)
        for part in range(2):
            give_far(i, part, 2, 3)
            start_halves(i, part)
        terms(i, 0)
        for part in range(2):
            give_far(i, part, 1, 0)

    def start_rest(i):
        give_far(i, 1, 2)
        start_halves(i, 1)
        give_far(i, 1, 3, 1, 0)

    def pass_on(i, part):
        take_far(i, part, 1, 3)
        span = near(part, i)
        if span[1]:
            land, rest = slot_half(part, i), pl.ds(*span)
            s_sem, r_sem = sq_s.at[part, i], sq_r.at[part, i]
            up, down = halves[part, i]
            up.wait_recv()
            add_into(i, at(1, bottom(span)), rq_half.at[i, 0, land])
            a = send(grad.at[i, at(1, span)], rq.at[i, 0, rest], s_sem.at[2], r_sem.at[2], q_up)
            down.wait_recv()
            add_into(i, at(3, top(span)), rq_half.at[i, 1, land])
            b = send(grad.at[i, at(3, span)], rq.at[i, 1, rest], s_sem.at[3], r_sem.at[3], q_down)
            wholes[part, i] = a, b

    def settle(i, part):
        span = near(part, i)
        if not span[1]:
            return
        for copy in wholes[part, i]:
            copy.wait_recv()
        dp, dx = i // 2, i % 2
        rest = pl.ds(*span)
        own = at(0, span)
        land = slot_half(part, i)
        up, down = p_up, p_down
        if dx:
            add_into(i, own, rq.at[i, 0, rest], rq.at[i, 1, rest])
            sx[part, dp] = send(
                grad.at[i, own], rx.at[dp, rest], sx_s.at[part, dp], sx_r.at[part, dp], x_other
            )
        elif dp == 2:
            take_far(4, part, 0)
            add_into(i, own, rq.at[i, 0, rest], rq.at[i, 1, rest])
            crossed = near(part, 5)
            if crossed[1]:
                sx[part, 2].wait_recv()
                add_into(i, at(0, crossed), rx.at[2, pl.ds(*crossed)])
            p_half[part, 0] = send(
                grad.at[i, at(0, bottom(span))], rp_half.at[0, land], sp_s.at[part, 0], sp_r.at[part, 0], up
            )
            p_half[part, 1] = send(
                grad.at[i, at(0, top(span))], rp_half.at[1, land], sp_s.at[part, 1], sp_r.at[part, 1], down
            )
        elif dp:
            sx[part, dp].wait_recv()
            add_into(i, own, rq.at[i, 0, rest], rq.at[i, 1, rest], rx.at[dp, rest])
            k = dp // 2
            p_half[part, k].wait_recv()
            add_into(i, at(0, (bottom, top)[k](span)), rp_half.at[k, land])
            p_whole[part, k] = send(
                grad.at[i, own], rp.at[k, rest], sp_s.at[part, 2 + k], sp_r.at[part, 2 + k], (up, down)[k]
            )

    def step_rows(part):
        span = near(part, 0)
        rest = pl.ds(*span)
        for copy in wholes[part, 0]:
            copy.wait_recv()
        sx[part, 0].wait_recv()
        total = grad[0, at(0, span)].astype(F32)
        for term in (rq.at[0, 0], rq.at[0, 1], rx.at[0]):
            total = total + term[rest].astype(F32)
        for k in (1, 0):
            p_whole[part, k].wait_recv()
            total = total + rp[k, rest].astype(F32)
        stepped_out[rest] = rolled[rest] - total

    pad = rows_out.shape[1]
    part_width = vocab // 4
    exchange, spread = [], []

    def my_columns(who):
        return pl.ds(pl.multiple_of(who * part_width, part_width), part_width)

    def start_sync():
        step_rows(0)
        for k in range(4):
            rows_out[k] = stepped_out[pl.ds(0, pad), k * part_width : (k + 1) * part_width]
        for j, to in enumerate(siblings):
            exchange.append(send(rows_out.at[to[0]], rows_in.at[j], e_s.at[j], e_r.at[j], to))

    def turn_sync():
        held = roll_up(anchor[...])[:pad]
        summed = rows_out[r]
        for j, copy in enumerate(exchange):
            copy.wait_recv()
            summed = summed + rows_in[j]
        delta = held - summed / 4
        moment = 0.9 * roll_up(momentum[...])[:pad] + delta
        moment_out[...] = moment
        fresh_rows = held - 0.7 * (delta + 0.9 * moment)
        new_out[...] = fresh_rows
        for j, to in enumerate(siblings):
            spread.append(send(new_out, new_in.at[j], n_s.at[j], n_r.at[j], to))
        fresh_out[:, my_columns(r)] = fresh_rows

    def end_sync():
        for j, copy in enumerate(spread):
            copy.wait_recv()
            fresh_out[:, my_columns(siblings[j][0])] = new_in[j]

    act = {
        "T": start_terms,
        "h": start_rest,
        "Z": start_both,
        "P": lambda i: pass_on(i, 0),
        "S": lambda i: settle(i, 0),
        "p": lambda i: pass_on(i, 1),
        "s": lambda i: settle(i, 1),
        "X": lambda i: (start_sync, turn_sync, end_sync)[i](),
    }
    for step in PLAN:
        act[step[0]](int(step[1]))
    step_rows(1)
    for copy in sent:
        copy.wait_send()


def merge(
    loss, stepped, fresh, moment, momentum, step_index, frag_table, loss_out, weights_out, momentum_out, rolled
):
    frag_count = frag_table.shape[0]
    rows = stepped.shape[0]
    run = rows // frag_count
    pad = fresh.shape[0]
    pos = step_index[0] % frag_count
    frag = jnp.int32(0)
    for k in range(frag_count):
        frag = frag + jnp.where(pos == k, frag_table[k], 0)
    offset = pl.multiple_of(frag * run // 8 * 8, 8)
    skip = frag * run - offset

    def synced(shape):
        row = lax.broadcasted_iota(jnp.int32, shape, 0)
        return (row >= skip) & (row < skip + run)

    loss_out[...] = loss[...]
    mixed = jnp.where(synced(fresh.shape), fresh[...], stepped[pl.ds(0, pad)])
    for k in range(2):
        rolled[pl.ds(k * rows, pad)] = mixed
        rolled[pl.ds(k * rows + pad, rows - pad)] = stepped[pl.ds(pad, rows - pad)]
    weights_out[...] = rolled[pl.ds(pl.multiple_of((rows - offset) % rows, 8), rows)]
    momentum_out[...] = momentum[...]
    momentum_out[pl.ds(offset, pad)] = jnp.where(synced(moment.shape), moment[...], momentum[pl.ds(offset, pad)])


def on_device(tokens, targets, norm_gain, weights, anchor, momentum, step_index, frag_table):
    _, count, width = tokens.shape
    _, rows, vocab = weights.shape
    half = rows // 2
    part = vocab // 4
    run = rows // frag_table.shape[0]
    pad = -(-run // 8) * 8
    vmem = pl.BlockSpec(memory_space=pltpu.VMEM)
    smem = pl.BlockSpec(memory_space=pltpu.SMEM)
    dma = pltpu.SemaphoreType.DMA
    big = pltpu.VMEM((8, 4 * rows, vocab), BF16)
    shapes = (
        jax.ShapeDtypeStruct((1, count), F32),
        jax.ShapeDtypeStruct((rows, vocab), F32),
        jax.ShapeDtypeStruct((rows, part), F32),
    )
    loss, stepped, fresh, moment = pl.pallas_call(
        kernel,
        out_shape=shapes[:2] + (jax.ShapeDtypeStruct((pad, vocab), F32), jax.ShapeDtypeStruct((pad, part), F32)),
        in_specs=[pl.BlockSpec(memory_space=pl.ANY)] * 8,
        out_specs=(vmem,) * 4,
        scratch_shapes=[
            big,
            pltpu.VMEM((8, 4 * rows, count), BF16),
            big,
            pltpu.VMEM((vocab, count), F32),
            pltpu.VMEM((vocab, count), BF16),
            pltpu.VMEM((2, 128, width), BF16),
            pltpu.VMEM((8, 2, half, vocab), BF16),
            pltpu.VMEM((8, 2, rows, vocab), BF16),
            pltpu.VMEM((4, rows, vocab), BF16),
            pltpu.VMEM((4, rows - NEAR, vocab), BF16),
            pltpu.VMEM((2, half, vocab), BF16),
            pltpu.VMEM((2, rows, vocab), BF16),
            pltpu.VMEM((rows, vocab), F32),
            pltpu.VMEM((4, pad, part), F32),
            pltpu.VMEM((3, pad, part), F32),
            pltpu.VMEM((pad, part), F32),
            pltpu.VMEM((3, pad, part), F32),
            pltpu.VMEM((1, count), jnp.int32),
            pltpu.VMEM((1, width), F32),
            pltpu.VMEM((rows, vocab), F32),
            pltpu.VMEM((rows, part), F32),
            pltpu.VMEM((rows, part), F32),
            pltpu.SMEM(step_index.shape, jnp.int32),
            pltpu.SMEM(frag_table.shape, jnp.int32),
            dma((7,)),
            dma((2,)),
            dma((4,)), dma((4,)), dma((4,)), dma((4,)), dma((4,)), dma((4,)), dma((8, 4)), dma((8, 4)),
            dma((2, 4)), dma((2, 4)), dma((2, 4)), dma((2, 4)), dma((2, 4)), dma((2, 4)), dma((2, 8, 4)), dma((2, 8, 4)),
            dma((3,)), dma((3,)), dma((3,)), dma((3,)),
        ],
        compiler_params=pltpu.CompilerParams(
            collective_id=0, has_side_effects=True, vmem_limit_bytes=62 * 1024 * 1024
        ),
    )(
        tokens, targets, norm_gain[None], weights[0], anchor, momentum, step_index, frag_table
    )
    loss, weights_out, momentum_out = pl.pallas_call(
        merge, out_shape=shapes, in_specs=[vmem] * 5 + [smem] * 2, out_specs=(vmem,) * 3,
        scratch_shapes=[pltpu.VMEM((2 * rows, vocab), F32)],
    )(loss, stepped, fresh, moment, momentum, step_index, frag_table)
    return (loss, weights_out[None], momentum_out)


def solution(mesh):
    return jax.shard_map(
        on_device,
        mesh=mesh,
        in_specs=(
            P("rep", "fsdp", None),
            P("rep", "fsdp"),
            P(),
            P("rep", "fsdp", None),
            P("fsdp", "rep"),
            P("fsdp", "rep"),
            P(),
            P(),
        ),
        out_specs=(P("rep", "fsdp"), P("rep", "fsdp", None), P("fsdp", "rep")),
        check_vma=False,
    )
```
